32 devices in a mesh: dp: 8 (over z, x), head: 4 (over y, core).
Axes of the slice: x: 2, y: 2, z: 4, core: 2. Of those that a mesh axis runs over, the one named last changes fastest.
Arguments:
- radar: bfloat16 [256, 136, 768], P(('dp', 'head')), may hold values from -6 to 6
- optical: bfloat16 [256, 136, 768], P(('dp', 'head')), may hold values from -6 to 6
- cotangent: bfloat16 [256, 136, 768], P(('dp', 'head')), may hold values from -6 to 6
- radar_ratio: int32 [256], P('dp'), may hold values from 40 to 90
- optical_ratio: int32 [256], P('dp'), may hold values from 40 to 90
- radar_patches: int32 [256, 136], P('dp'), may hold values from 0 to 224, as said below
- optical_patches: int32 [256, 136], P('dp'), may hold values from 0 to 224, as said below
- pairing: int32 [256], P('dp'), may hold values from 0 to 31, as said below
- norm_gain: bfloat16 [3, 768], replicated, may hold values from 0.5 to 1.5
- norm_bias: bfloat16 [3, 768], replicated, may hold values from -1.75 to 1.75
- self_qkv: bfloat16 [768, 2304], replicated, may hold values from -0.21875 to 0.21875
- self_out: bfloat16 [768, 768], replicated, may hold values from -0.875 to 0.875
- cross_q: bfloat16 [768, 768], replicated, may hold values from -0.21875 to 0.21875
- cross_kv: bfloat16 [768, 1536], replicated, may hold values from -0.21875 to 0.21875
- cross_out: bfloat16 [768, 768], replicated, may hold values from -0.875 to 0.875
- mlp_in: bfloat16 [768, 3072], replicated, may hold values from -0.21875 to 0.21875
- mlp_in_bias: bfloat16 [3072], replicated, may hold values from -3 to 3
- mlp_out: bfloat16 [3072, 768], replicated, may hold values from -0.109375 to 0.109375
- mlp_out_bias: bfloat16 [768], replicated, may hold values from -1.75 to 1.75
Outputs:
- mixed: bfloat16 [256, 136, 768], P(('dp', 'head'))
- radar_grad: bfloat16 [256, 136, 768], P(('dp', 'head'))
- optical_grad: bfloat16 [256, 136, 768], P(('dp', 'head'))
- norm_gain_grad: bfloat16 [3, 768], replicated
- norm_bias_grad: bfloat16 [3, 768], replicated
- self_qkv_grad: bfloat16 [768, 2304], replicated
- self_out_grad: bfloat16 [768, 768], replicated
- cross_q_grad: bfloat16 [768, 768], replicated
- cross_kv_grad: bfloat16 [768, 1536], replicated
- cross_out_grad: bfloat16 [768, 768], replicated
- mlp_in_grad: bfloat16 [768, 3072], replicated
- mlp_in_bias_grad: bfloat16 [3072], replicated
- mlp_out_grad: bfloat16 [3072, 768], replicated
- mlp_out_bias_grad: bfloat16 [768], replicated
The draws below stay inside these ranges and needn't reach their ends.
Inputs may be any that keep to these rules, and one draw needn't show every extreme that they name: `radar_patches`: each row holds distinct patch numbers of the 15 x 15 grid in row-major order; slot a holds a visible patch when a is below the image's visible count. `optical_patches`: each row holds distinct patch numbers of the 15 x 15 grid in row-major order; slot a holds a visible patch when a is below the image's visible count. Within each aligned block of 32 images the values are a permutation of the block's places: radar image b is paired with optical image 32 * (b // 32) + pairing[b].
All inputs are finite; a program needn't handle non-finite values.
Results may differ from the reference program's by a relative error of at most 0.019.
Values may be sent and summed in bfloat16 or wider, within the bound.
No kernel may reach another device: no remote copies, remote signals or barrier semaphores. Data moves between devices by JAX's collectives and lax.ppermute only.
A program may use at most 320 MiB of HBM per device.

```python
import math
import jax
import jax.numpy as jnp
from jax import lax

D = 768
HEADS = 12
HEAD_DIM = 64
FF = 3072
GRID = 15
SLOTS = 136
GROUP_IMG = 32
IMAGES = 256


def ratio_draw(base_key):
    ratios = jax.random.randint(base_key, (IMAGES,), 40, 91)
    spots = jax.random.permutation(jax.random.fold_in(base_key, 7), IMAGES)
    places = jnp.arange(IMAGES)
    ratios = jnp.where(places == spots[0], 40, ratios)
    return jnp.where(places == spots[1], 90, ratios).astype(jnp.int32)


def patch_draw(base_key):
    keys = jax.random.split(base_key, IMAGES)

    def shuffle_one(single_key):
        return jax.random.permutation(single_key, GRID * GRID)[:SLOTS]
    return jax.vmap(shuffle_one)(keys).astype(jnp.int32)


def draw_radar_ratio(key, part):
    key = jax.random.fold_in(key, 11)
    return ratio_draw(key)


def draw_optical_ratio(key, part):
    key = jax.random.fold_in(key, 12)
    return ratio_draw(key)


def draw_radar_patches(key, part):
    key = jax.random.fold_in(key, 13)
    return patch_draw(key)


def draw_optical_patches(key, part):
    key = jax.random.fold_in(key, 14)
    return patch_draw(key)


def draw_pairing(key, part):
    key = jax.random.fold_in(key, 15)
    keys = jax.random.split(key, IMAGES // GROUP_IMG)

    def shuffle_block(single_key):
        return jax.random.permutation(single_key, GROUP_IMG)
    return jax.vmap(shuffle_block)(keys).reshape(IMAGES).astype(jnp.int32)


def steps_of(rng, dims, cuts, smallest, largest):
    def one(position, shards_of):
        heights = jax.random.uniform(jax.random.fold_in(jax.random.fold_in(rng, 6), position), (shards_of,), jnp.float32, smallest / len(cuts), largest / len(cuts))
        return jnp.repeat(jnp.exp(heights), dims[position] // shards_of).reshape((-1,) + (1,) * (len(dims) - position - 1))

    level = one(*cuts[0])
    for cut in cuts[1:]:
        level = level * one(*cut)
    return level


def gaussian(stream_key, shape, scale, most, cuts=(), kind=jnp.bfloat16):
    factor_of = steps_of(stream_key, shape, cuts, -0.22, 0.18) if cuts else 1.0
    entries = jax.random.normal(stream_key, shape, jnp.float32) * scale * factor_of
    return jnp.minimum(jnp.maximum(entries, -most), most).astype(kind)


def setup_inputs(seed: int = 0) -> dict:
    streams_of = jax.random.split(jax.random.key(seed), 20)
    radar = gaussian(streams_of[0], (IMAGES, SLOTS, D), 1.0, 6.0, ((0, 32),))
    optical = gaussian(streams_of[1], (IMAGES, SLOTS, D), 1.0, 6.0, ((0, 32),))
    cotangent = gaussian(streams_of[2], (IMAGES, SLOTS, D), 1.0, 6.0, ((0, 32),))
    radar_ratio = draw_radar_ratio(jax.random.fold_in(streams_of[19], 71), 0)
    optical_ratio = draw_optical_ratio(jax.random.fold_in(streams_of[19], 71), 0)
    radar_patches = draw_radar_patches(jax.random.fold_in(streams_of[19], 71), 0)
    optical_patches = draw_optical_patches(jax.random.fold_in(streams_of[19], 71), 0)
    pairing = draw_pairing(jax.random.fold_in(streams_of[19], 71), 0)
    norm_gain = jnp.clip(1.0 + 0.1 * jax.random.normal(streams_of[8], (3, D), jnp.float32), 0.5, 1.5).astype(jnp.bfloat16)
    norm_bias = gaussian(streams_of[9], (3, D), 0.3, 1.75)
    self_qkv = gaussian(streams_of[10], (D, 3 * D), D ** -0.5, 0.21875)
    self_out = gaussian(streams_of[11], (D, D), (D // 16) ** -0.5, 0.875)
    cross_q = gaussian(streams_of[12], (D, D), D ** -0.5, 0.21875)
    cross_kv = gaussian(streams_of[13], (D, 2 * D), D ** -0.5, 0.21875)
    cross_out = gaussian(streams_of[14], (D, D), (D // 16) ** -0.5, 0.875)
    mlp_in = gaussian(streams_of[15], (D, FF), D ** -0.5, 0.21875)
    mlp_in_bias = gaussian(streams_of[16], (FF,), 0.5, 3.0)
    mlp_out = gaussian(streams_of[17], (FF, D), FF ** -0.5, 0.109375)
    mlp_out_bias = gaussian(streams_of[18], (D,), 0.3, 1.75)
    return dict(radar=radar, optical=optical, cotangent=cotangent, radar_ratio=radar_ratio, optical_ratio=optical_ratio, radar_patches=radar_patches, optical_patches=optical_patches, pairing=pairing, norm_gain=norm_gain, norm_bias=norm_bias, self_qkv=self_qkv, self_out=self_out, cross_q=cross_q, cross_kv=cross_kv, cross_out=cross_out, mlp_in=mlp_in, mlp_in_bias=mlp_in_bias, mlp_out=mlp_out, mlp_out_bias=mlp_out_bias)


@jax.custom_vjp
def low(v):
    return lax.optimization_barrier(v.astype(jnp.bfloat16)).astype(jnp.float32)

@jax.custom_vjp
def low_back(v):
    return v

def low_keep(v):
    return (low(v), None)

def low_pass(kept, grad):
    return (grad,)

def back_keep(v):
    return (v, None)

def back_low(kept, grad):
    return (low(grad),)
low.defvjp(low_keep, low_pass)
low_back.defvjp(back_keep, back_low)

def rounded(values):
    return low_back(low(values))

def visible_count(ratio):
    return GRID * GRID * (100 - ratio) // 100

def head_slopes():
    return 2.0 ** (-8.0 * (jnp.arange(HEADS, dtype=jnp.float32) + 1.0) / HEADS)

def patch_distance(query_patch, key_patch):
    query_row = (query_patch // GRID).astype(jnp.float32)
    query_column = (query_patch % GRID).astype(jnp.float32)
    key_row = (key_patch // GRID).astype(jnp.float32)
    key_column = (key_patch % GRID).astype(jnp.float32)
    delta_row = query_row[..., :, None] - key_row[..., None, :]
    delta_column = query_column[..., :, None] - key_column[..., None, :]
    return jnp.sqrt(delta_row * delta_row + delta_column * delta_column)

def product(left, right):
    return jnp.dot(left, right, precision=lax.Precision.HIGHEST, preferred_element_type=jnp.float32)

def layer_norm(values, gain, shift):
    centre = values - lax.optimization_barrier(jnp.mean(values, axis=-1, keepdims=True))
    spread = lax.optimization_barrier(jnp.mean(centre * centre, axis=-1, keepdims=True))
    return centre * lax.rsqrt(spread + 1e-06) * gain + shift

def attend(query, keys, values, bias, live_keys):
    scale = 1.0 / math.sqrt(HEAD_DIM)
    scores = jnp.einsum('bqhd,bkhd->bhqk', query, keys, precision=lax.Precision.HIGHEST) * scale + bias
    scores = low_back(scores)
    scores = jnp.where(live_keys[:, None, None, :], scores, -1e+30)
    weights = jax.nn.softmax(scores, axis=-1)
    return jnp.einsum('bhqk,bkhd->bqhd', low(weights), values, precision=lax.Precision.HIGHEST)

def block_forward(weights, radar_block, optical_block, radar_live, optical_live, radar_patch, optical_patch, partner):
    norm_gain, norm_bias, self_qkv, self_out, cross_q, cross_kv, cross_out, mlp_in, mlp_in_bias, mlp_out, mlp_out_bias = weights
    images, slots, width = radar_block.shape
    slopes = head_slopes()
    normed = low(layer_norm(radar_block, norm_gain[0], norm_bias[0]))
    packed = rounded(product(normed, self_qkv)).reshape(images, slots, 3, HEADS, HEAD_DIM)
    self_bias = -slopes[None, :, None, None] * patch_distance(radar_patch, radar_patch)[:, None]
    self_mixed = rounded(attend(packed[:, :, 0], packed[:, :, 1], packed[:, :, 2], self_bias, radar_live))
    first = radar_block + low_back(product(self_mixed.reshape(images, slots, width), self_out))
    normed = low(layer_norm(first, norm_gain[1], norm_bias[1]))
    query = rounded(product(normed, cross_q)).reshape(images, slots, HEADS, HEAD_DIM)
    context = rounded(product(optical_block, cross_kv))[partner].reshape(images, slots, 2, HEADS, HEAD_DIM)
    cross_bias = -slopes[None, :, None, None] * patch_distance(radar_patch, optical_patch[partner])[:, None]
    cross_mixed = rounded(attend(query, context[:, :, 0], context[:, :, 1], cross_bias, optical_live[partner]))
    second = first + low_back(product(cross_mixed.reshape(images, slots, width), cross_out))
    normed = low(layer_norm(second, norm_gain[2], norm_bias[2]))
    inner = low_back(product(normed, mlp_in) + mlp_in_bias)
    activated = rounded(jax.nn.gelu(inner, approximate=False))
    output = second + low_back(product(activated, mlp_out) + mlp_out_bias)
    return jnp.where(radar_live[:, :, None], output, 0.0)

def reference(radar, optical, cotangent, radar_ratio, optical_ratio, radar_patches, optical_patches, pairing, norm_gain, norm_bias, self_qkv, self_out, cross_q, cross_kv, cross_out, mlp_in, mlp_in_bias, mlp_out, mlp_out_bias):
    weights = tuple((weight.astype(jnp.float32) for weight in (norm_gain, norm_bias, self_qkv, self_out, cross_q, cross_kv, cross_out, mlp_in, mlp_in_bias, mlp_out, mlp_out_bias)))
    blocks = IMAGES // GROUP_IMG

    def split(values):
        return values.reshape((blocks, GROUP_IMG) + values.shape[1:])
    slot_ids = jnp.arange(SLOTS, dtype=jnp.int32)
    radar_live = split(slot_ids[None, :] < visible_count(radar_ratio)[:, None])
    optical_live = split(slot_ids[None, :] < visible_count(optical_ratio)[:, None])
    radar_patch = split(radar_patches)
    optical_patch = split(optical_patches)
    partner = split(pairing)

    def forward(weight_set, radar_full, optical_full):

        def one_block(inputs):
            return block_forward(weight_set, *inputs)
        outputs = lax.map(jax.checkpoint(one_block), (split(radar_full), split(optical_full), radar_live, optical_live, radar_patch, optical_patch, partner))
        return outputs.reshape(radar_full.shape)
    output, backward = jax.vjp(forward, weights, radar.astype(jnp.float32), optical.astype(jnp.float32))
    grads, radar_grad, optical_grad = backward(cotangent.astype(jnp.float32))
    return (output.astype(jnp.bfloat16), radar_grad.astype(jnp.bfloat16), optical_grad.astype(jnp.bfloat16), grads[0].astype(jnp.bfloat16), grads[1].astype(jnp.bfloat16), grads[2].astype(jnp.bfloat16), grads[3].astype(jnp.bfloat16), grads[4].astype(jnp.bfloat16), grads[5].astype(jnp.bfloat16), grads[6].astype(jnp.bfloat16), grads[7].astype(jnp.bfloat16), grads[8].astype(jnp.bfloat16), grads[9].astype(jnp.bfloat16), grads[10].astype(jnp.bfloat16))
```

```python
from functools import partial
import math

import jax
import jax.numpy as jnp
from jax import lax
from jax.experimental import pallas as pl
from jax.experimental.pallas import tpu as pltpu
from jax.sharding import PartitionSpec as P

HEADS = 12
HEAD_DIM = 64
GRID = 15
PAIR = 2
QUAD = 4
WIDE = QUAD * HEAD_DIM
FAR = 1e15
VMEM_BYTES = 61 * 1024 * 1024
SLOPES = [2.0 ** (-8.0 * (h + 1.0) / HEADS) for h in range(HEADS)]
SCALE = 1.0 / math.sqrt(HEAD_DIM)
F32 = jnp.float32
BF16 = jnp.bfloat16
SMALL_COST = pl.CostEstimate(flops=1, bytes_accessed=1, transcendentals=0)


def mm(left, right):
    return jnp.dot(left, right, preferred_element_type=F32)


def mm_t(left, right):
    return lax.dot_general(left, right, (((1,), (1,)), ((), ())), preferred_element_type=F32)


def t_mm(left, right):
    return lax.dot_general(left, right, (((0,), (0,)), ((), ())), preferred_element_type=F32)


def rows_of(ref):
    value = ref[...].astype(F32)
    return value.reshape(value.shape[0] * value.shape[1], value.shape[2])


def put_rows(ref, value):
    slots = ref.shape[1]
    for i in range(ref.shape[0]):
        ref[i] = value[i * slots : (i + 1) * slots].astype(ref.dtype)


def norm(values):
    centre = values - jnp.mean(values, axis=-1, keepdims=True)
    inverse = lax.rsqrt(jnp.mean(centre * centre, axis=-1, keepdims=True) + 1e-6)
    return centre * inverse, inverse


def norm_back(grad, scaled, inverse, gain):
    weighted = grad * gain
    return inverse * (
        weighted
        - jnp.mean(weighted, axis=-1, keepdims=True)
        - scaled * jnp.mean(weighted * scaled, axis=-1, keepdims=True)
    )


def column_sum(values):
    return jnp.sum(values, axis=0, keepdims=True)


def head_masks(dtype):
    lane = lax.broadcasted_iota(jnp.int32, (1, WIDE), 1) // HEAD_DIM
    return [(lane == h).astype(F32).astype(dtype) for h in range(QUAD)]


def as_column(row, slots):
    n = row.shape[1]
    same = lax.broadcasted_iota(jnp.int32, (slots, n), 0) == lax.broadcasted_iota(
        jnp.int32, (slots, n), 1
    )
    return jnp.sum(jnp.where(same, jnp.broadcast_to(row, (slots, n)), 0.0), axis=1, keepdims=True)


def distances(query_pos, key_pos, slots, keys):
    delta_row = as_column(query_pos[0:1], slots) - key_pos[0:1, :keys]
    delta_column = as_column(query_pos[1:2], slots) - key_pos[1:2, :keys]
    return jnp.sqrt(delta_row * delta_row + delta_column * delta_column)


def stacked(block, keys, masks):
    slots = block.shape[0]
    if keys <= slots:
        part = block[:keys]
    else:
        part = jnp.concatenate(
            (block.astype(F32), jnp.zeros((keys - slots, block.shape[1]), F32)), axis=0
        ).astype(BF16)
    return jnp.concatenate([part * m for m in masks], axis=0)


def attend(i, keys, q_of, k_of, v_of, query_pos, key_pos, p_ref, o_ref):
    slots = o_ref.shape[1]
    dist = distances(query_pos, key_pos, slots, keys)
    masks = head_masks(BF16)
    for g in range(HEADS // QUAD):
        q = q_of(g) * jnp.asarray(SCALE, BF16)
        scores = mm_t(q, stacked(k_of(g), keys, masks))
        parts = []
        for h in range(QUAD):
            s = scores[:, h * keys : (h + 1) * keys] - SLOPES[g * QUAD + h] * dist
            e = jnp.exp(s - jnp.max(s, axis=1, keepdims=True))
            parts.append((e * (1.0 / jnp.sum(e, axis=1, keepdims=True))).astype(BF16))
        p = jnp.concatenate(parts, axis=1)
        p_ref[i, :, g * QUAD * keys : (g + 1) * QUAD * keys] = p
        o_ref[i, :, g * WIDE : (g + 1) * WIDE] = mm(p, stacked(v_of(g), keys, masks)).astype(BF16)


def attend_back(i, keys, q_of, k_of, v_of, do_of, p_ref, put_dq, put_dk, put_dv, slots):
    masks = head_masks(BF16)
    wide_masks = head_masks(F32)

    def gathered(product):
        total = sum(product[h * keys : (h + 1) * keys] * wide_masks[h] for h in range(QUAD))
        if keys >= slots:
            return total[:slots]
        return jnp.concatenate((total, jnp.zeros((slots - keys, WIDE), F32)), axis=0)

    for g in range(HEADS // QUAD):
        q, do = q_of(g), do_of(g)
        keys_stack = stacked(k_of(g), keys, masks)
        dp = mm_t(do, stacked(v_of(g), keys, masks))
        p = p_ref[i, :, g * QUAD * keys : (g + 1) * QUAD * keys]
        parts = []
        for h in range(QUAD):
            ph = p[:, h * keys : (h + 1) * keys].astype(F32)
            t = ph * dp[:, h * keys : (h + 1) * keys]
            parts.append((t - ph * jnp.sum(t, axis=1, keepdims=True)).astype(BF16))
        ds = jnp.concatenate(parts, axis=1)
        put_dv(g, gathered(t_mm(p, do)).astype(BF16))
        put_dq(g, (mm(ds, keys_stack) * SCALE).astype(BF16))
        put_dk(g, (gathered(t_mm(ds, q)) * SCALE).astype(BF16))


def by_count(count, slots, work):
    small = min(slots, 128)
    pl.when(count <= small)(lambda: work(small))
    if slots > small:
        pl.when(count > small)(lambda: work(256))


def gelu_parts(u):
    size = jnp.abs(u)
    t = 1.0 / (1.0 + (0.3275911 / math.sqrt(2.0)) * size)
    poly = 0.5 * 1.061405429
    for c in (-1.453152027, 1.421413741, -0.284496736, 0.254829592):
        poly = poly * t + 0.5 * c
    bell = jnp.exp(-0.5 * (u * u))
    tail = poly * t * bell
    phi_cap = jnp.where(u >= 0.0, 1.0 - tail, tail)
    return u * phi_cap, phi_cap + u * (bell * (1.0 / math.sqrt(2.0 * math.pi)))


def live_rows(counts, slots):
    slot = lax.broadcasted_iota(jnp.int32, (slots, 1), 0)
    return jnp.concatenate([(slot < c).astype(F32) for c in counts], axis=0)


def self_forward(
    count, x_ref, pos_ref, gain_ref, shift_ref, qkv_w, out_w, q_w,
    h1_ref, qkv_ref, p_ref, o_ref, x1_ref, h2_ref, q2_ref,
):
    step = pl.program_id(0)
    pair, slots, width = x_ref.shape
    x = rows_of(x_ref)
    scaled, _ = norm(x)
    h1 = (scaled * gain_ref[0:1] + shift_ref[0:1]).astype(BF16)
    put_rows(h1_ref, h1.astype(F32))
    put_rows(qkv_ref, mm(h1, qkv_w[...]))
    for i in range(pair):

        def block(kind, i=i):
            return lambda g: qkv_ref[i, :, kind * width + g * WIDE : kind * width + (g + 1) * WIDE]

        by_count(
            count[step * pair + i],
            slots,
            lambda keys, i=i, block=block: attend(
                i, keys, block(0), block(1), block(2), pos_ref[i], pos_ref[i], p_ref, o_ref
            ),
        )
    x1 = x + mm(rows_of(o_ref).astype(BF16), out_w[...])
    put_rows(x1_ref, x1)
    scaled, _ = norm(x1)
    h2 = (scaled * gain_ref[1:2] + shift_ref[1:2]).astype(BF16)
    put_rows(h2_ref, h2.astype(F32))
    put_rows(q2_ref, mm(h2, q_w[...]))


def cross_and_mlp(
    count, other_count, x1_ref, q2_ref, opt_ref, dy_ref, pos_ref, other_pos_ref, gain_ref, shift_ref,
    kv_w, out_w, in_w, in_b, mo_w, mo_b,
    mixed_ref, kv_ref, p_ref, o_ref, h3_ref, g_ref, du_ref, dm_ref, dx2_ref, sums_ref, in_sums_ref,
):
    step = pl.program_id(0)
    pair, slots, width = x1_ref.shape
    hidden = in_w.shape[1]
    put_rows(kv_ref, mm(rows_of(opt_ref).astype(BF16), kv_w[...]))
    for i in range(pair):

        def block(ref, kind, i=i):
            return lambda g: ref[i, :, kind * width + g * WIDE : kind * width + (g + 1) * WIDE]

        by_count(
            other_count[step * pair + i],
            slots,
            lambda keys, i=i, block=block: attend(
                i, keys, block(q2_ref, 0), block(kv_ref, 0), block(kv_ref, 1),
                pos_ref[i], other_pos_ref[i], p_ref, o_ref,
            ),
        )
    x2 = rows_of(x1_ref) + mm(rows_of(o_ref).astype(BF16), out_w[...])
    scaled, inverse = norm(x2)
    gain = gain_ref[2:3]
    h3 = (scaled * gain + shift_ref[2:3]).astype(BF16)
    put_rows(h3_ref, h3.astype(F32))
    live = live_rows([count[step * pair + i] for i in range(pair)], slots)
    dy = rows_of(dy_ref) * live
    dm = dy.astype(BF16)
    put_rows(dm_ref, dy)
    chunk = 768
    g_parts, du_parts, in_sums = [], [], []
    for j in range(hidden // chunk):
        cols = slice(j * chunk, (j + 1) * chunk)
        u = mm(h3, in_w[:, cols]) + in_b[0:1, cols]
        dg = mm_t(dm, mo_w[cols, :]).astype(BF16).astype(F32)
        g, slope = gelu_parts(u)
        du = dg * slope
        for i in range(pair):
            rows = slice(i * slots, (i + 1) * slots)
            g_ref[i, :, cols] = g[rows].astype(BF16)
            du_ref[i, :, cols] = du[rows].astype(BF16)
        g_parts.append(g.astype(BF16))
        du_parts.append(du.astype(BF16))
        in_sums.append(column_sum(du.astype(BF16).astype(F32)))
    y = x2 + (mm(jnp.concatenate(g_parts, axis=1), mo_w[...]) + mo_b[0:1])
    put_rows(mixed_ref, y * live)
    dh3 = mm_t(jnp.concatenate(du_parts, axis=1), in_w[...])
    put_rows(dx2_ref, dy + norm_back(dh3, scaled, inverse, gain))
    sums = jnp.concatenate((column_sum(dh3 * scaled), column_sum(dh3), column_sum(dy)), axis=0)
    in_sums = jnp.concatenate(in_sums, axis=1)

    @pl.when(step == 0)
    def _():
        sums_ref[...] = sums
        in_sums_ref[...] = in_sums

    @pl.when(step > 0)
    def _():
        sums_ref[...] += sums
        in_sums_ref[...] += in_sums


def cross_back(
    other_count, dx2_ref, x1_ref, q2_ref, kv_ref, p_ref, gain_ref, out_w, q_w, kv_w,
    da2_ref, dq2_ref, dkv_ref, og_ref, dx1_ref, sums_ref, do_ref,
):
    step = pl.program_id(0)
    pair, slots, width = x1_ref.shape
    dx2 = rows_of(dx2_ref)
    da2 = dx2.astype(BF16)
    put_rows(da2_ref, dx2)
    put_rows(do_ref, mm_t(da2, out_w[...]))
    for i in range(pair):

        def block(ref, kind, i=i):
            return lambda g: ref[i, :, kind * width + g * WIDE : kind * width + (g + 1) * WIDE]

        def put(ref, kind, i=i):
            def store(g, value):
                ref[i, :, kind * width + g * WIDE : kind * width + (g + 1) * WIDE] = value

            return store

        by_count(
            other_count[step * pair + i],
            slots,
            lambda keys, i=i, block=block, put=put: attend_back(
                i, keys, block(q2_ref, 0), block(kv_ref, 0), block(kv_ref, 1), block(do_ref, 0),
                p_ref, put(dq2_ref, 0), put(dkv_ref, 0), put(dkv_ref, 1), slots,
            ),
        )
    put_rows(og_ref, mm_t(rows_of(dkv_ref).astype(BF16), kv_w[...]))
    dh2 = mm_t(rows_of(dq2_ref).astype(BF16), q_w[...])
    scaled, inverse = norm(rows_of(x1_ref))
    put_rows(dx1_ref, dx2 + norm_back(dh2, scaled, inverse, gain_ref[1:2]))
    sums = jnp.concatenate((column_sum(dh2 * scaled), column_sum(dh2)), axis=0)

    @pl.when(step == 0)
    def _():
        sums_ref[...] = sums

    @pl.when(step > 0)
    def _():
        sums_ref[...] += sums


def self_back(
    count, dx1_ref, x_ref, qkv_ref, p_ref, gain_ref, out_w, qkv_w,
    dqkv_ref, dx_ref, sums_ref, do_ref,
):
    step = pl.program_id(0)
    pair, slots, width = x_ref.shape
    dx1 = rows_of(dx1_ref)
    da1 = dx1.astype(BF16)
    put_rows(do_ref, mm_t(da1, out_w[...]))
    for i in range(pair):

        def block(ref, kind, i=i):
            return lambda g: ref[i, :, kind * width + g * WIDE : kind * width + (g + 1) * WIDE]

        def put(ref, kind, i=i):
            def store(g, value):
                ref[i, :, kind * width + g * WIDE : kind * width + (g + 1) * WIDE] = value

            return store

        by_count(
            count[step * pair + i],
            slots,
            lambda keys, i=i, block=block, put=put: attend_back(
                i, keys, block(qkv_ref, 0), block(qkv_ref, 1), block(qkv_ref, 2), block(do_ref, 0),
                p_ref, put(dqkv_ref, 0), put(dqkv_ref, 1), put(dqkv_ref, 2), slots,
            ),
        )
    dh1 = mm_t(rows_of(dqkv_ref).astype(BF16), qkv_w[...])
    scaled, inverse = norm(rows_of(x_ref))
    put_rows(dx_ref, dx1 + norm_back(dh1, scaled, inverse, gain_ref[0:1]))
    sums = jnp.concatenate((column_sum(dh1 * scaled), column_sum(dh1)), axis=0)

    @pl.when(step == 0)
    def _():
        sums_ref[...] = sums

    @pl.when(step > 0)
    def _():
        sums_ref[...] += sums


def take_images(source, place, *refs):
    j = pl.program_id(0)
    for r, ref in enumerate(refs[:-1]):

        @pl.when(source[j] == r)
        def _(ref=ref):
            refs[-1][...] = ref[...]


def pack_blocks(core, *refs):
    count = (len(refs) - 2) // 2
    for first, out in ((0, refs[-2]), (count, refs[-1])):
        column = 0
        for ref in refs[first : first + count]:
            out[:, column : column + ref.shape[1]] = ref[...]
            column += ref.shape[1]


def unpack_blocks(core, own, other, *outs):
    def copy(source):
        column = 0
        for out in outs:
            out[...] = source[:, column : column + out.shape[1]]
            column += out.shape[1]

    pl.when(pl.program_id(0) == core[0])(lambda: copy(own))
    pl.when(pl.program_id(0) != core[0])(lambda: copy(other))


def add_blocks(bits, *refs):
    third = len(refs) // 3
    for one, other, out in zip(refs[:third], refs[third : 2 * third], refs[2 * third :]):
        value = (one[...].astype(F32) + other[...].astype(F32)).astype(out.dtype)
        out[...] = value.reshape(out.shape)


def merge_blocks(bits, *refs):
    third = len(refs) // 3
    half = pl.program_id(0)
    for p, (one, other, out) in enumerate(zip(refs[:third], refs[third : 2 * third], refs[2 * third :])):

        @pl.when(half == bits[p])
        def _(one=one, out=out):
            out[...] = one[...].reshape(out.shape)

        @pl.when(half != bits[p])
        def _(other=other, out=out):
            out[...] = other[...].reshape(out.shape)


def images_call(kernel, scalars, arrays, whole, outs, sums, scratch, flops, name):
    images = arrays[0].shape[0]
    pair = PAIR if images % PAIR == 0 else 1

    def split_spec(shape):
        rank = len(shape)
        return pl.BlockSpec((pair,) + tuple(shape[1:]), lambda i, *s: (i,) + (0,) * (rank - 1))

    def whole_spec(shape):
        rank = len(shape)
        return pl.BlockSpec(tuple(shape), lambda i, *s: (0,) * rank, pipeline_mode=pl.Buffered(1))

    out_shapes = [jax.ShapeDtypeStruct((images,) + tail, dtype) for tail, dtype in outs]
    sum_shapes = [jax.ShapeDtypeStruct(shape, F32) for shape in sums]
    moved = sum(x.size * x.dtype.itemsize for x in (*arrays, *whole, *out_shapes))
    return pl.pallas_call(
        kernel,
        grid_spec=pltpu.PrefetchScalarGridSpec(
            num_scalar_prefetch=len(scalars),
            grid=(images // pair,),
            in_specs=[split_spec(a.shape) for a in arrays] + [whole_spec(a.shape) for a in whole],
            out_specs=[split_spec(o.shape) for o in out_shapes]
            + [pl.BlockSpec(s.shape, lambda i, *_: (0, 0)) for s in sum_shapes],
            scratch_shapes=[pltpu.VMEM((pair,) + tail, dtype) for tail, dtype in scratch],
        ),
        out_shape=out_shapes + sum_shapes,
        compiler_params=pltpu.CompilerParams(vmem_limit_bytes=VMEM_BYTES),
        cost_estimate=SMALL_COST,
        name=name,
    )(*scalars, *arrays, *whole)


def take_call(source, place, sources):
    shape = sources[0].shape
    block = (1,) + shape[1:]

    def spec(r):
        return pl.BlockSpec(block, lambda j, source, place: (jnp.where(source[j] == r, place[j], 0), 0, 0))

    return pl.pallas_call(
        take_images,
        grid_spec=pltpu.PrefetchScalarGridSpec(
            num_scalar_prefetch=2,
            grid=(shape[0],),
            in_specs=[spec(r) for r in range(len(sources))],
            out_specs=pl.BlockSpec(block, lambda j, source, place: (j, 0, 0)),
        ),
        out_shape=jax.ShapeDtypeStruct(shape, sources[0].dtype),
        cost_estimate=SMALL_COST,
        name="take_images",
    )(source, place, *sources)


def plain_call(kernel, scalars, grid, ins, outs, name):
    shapes = [jax.ShapeDtypeStruct(shape, BF16) for shape, _, _ in outs]
    moved = 2 * (sum(math.prod(s.shape) for s in shapes) * 3)
    return pl.pallas_call(
        kernel,
        grid_spec=pltpu.PrefetchScalarGridSpec(
            num_scalar_prefetch=1,
            grid=(grid,),
            in_specs=[pl.BlockSpec(block, index) for _, block, index in ins],
            out_specs=[pl.BlockSpec(block, index) for _, block, index in outs],
        ),
        out_shape=shapes,
        compiler_params=pltpu.CompilerParams(vmem_limit_bytes=VMEM_BYTES),
        cost_estimate=SMALL_COST,
        name=name,
    )(scalars, *[a for a, _, _ in ins])


def bit_of(axis_name, bit):
    return (lax.axis_index(axis_name) // bit) % 2


PARTS = 3


def sum_levels():
    head, dp = lax.axis_size("head"), lax.axis_size("dp")
    links = [("head", 2**i) for i in reversed(range(1, head.bit_length() - 1))]
    links += [("dp", 2**i) for i in range(dp.bit_length() - 1)]
    turn = links[:PARTS] if len(links) >= PARTS else []
    levels = [[turn[(p + k) % PARTS] for p in range(PARTS)] for k in range(len(turn))]
    return levels + [[link] * PARTS for link in links[len(turn) :]]


def total_by_halves(mats):
    rows = mats[0].shape[0]
    widths = [m.shape[1] for m in mats]
    wide = sum(widths)
    levels = sum_levels()
    n = 2 ** len(levels)
    part_rows = rows // (2 * PARTS)
    r = part_rows // n
    core = bit_of("head", 1)[None].astype(jnp.int32)

    def mine(p, core):
        return (core[0] * PARTS + p, 0)

    def theirs(p, core):
        return ((1 - core[0]) * PARTS + p, 0)

    send, keep = plain_call(
        pack_blocks,
        core,
        PARTS,
        [(m, (part_rows, m.shape[1]), theirs) for m in mats] + [(m, (part_rows, m.shape[1]), mine) for m in mats],
        [((PARTS * part_rows, wide), (part_rows, wide), lambda p, core: (p, 0))] * 2,
        "pack_blocks",
    )
    got = [flip(send.reshape(PARTS, n, r, wide), "head", 1)]
    keep = [keep.reshape(PARTS, n, r, wide)]

    def is_stacked(arrays):
        return len(arrays) == 1

    def split_step(keep, got, bits, same, n):
        half = n // 2
        chunk = min(half, 2)

        def reader(arrays, p, other):
            def index(i, bits):
                b = 1 - bits[p] if other else bits[p]
                return b * (half // chunk) + i

            if is_stacked(arrays):
                return (arrays[0], (1, chunk, r, wide), lambda i, bits: (p, index(i, bits), 0, 0))
            return (arrays[p], (chunk, r, wide), lambda i, bits: (index(i, bits), 0, 0))

        order = [(p, other) for other in (True, False) for p in range(PARTS)]
        ones = [reader(keep, p, other) for p, other in order]
        others = [reader(got, p, other) for p, other in order]
        outs = [((half, r, wide), (chunk, r, wide), lambda i, bits: (i, 0, 0))] * (2 * PARTS)
        done = plain_call(add_blocks, bits, half // chunk, ones + others, outs, "add_blocks")
        return list(done[:PARTS]), list(done[PARTS:])

    def level_bits(level):
        return jnp.stack([bit_of(*link) for link in level]).astype(jnp.int32)

    for level in levels:
        send, keep = split_step(keep, got, level_bits(level), False, n)
        n //= 2
        got = [flip(x, *link) for x, link in zip(send, level)]
    ones = [(x, (1, r, wide), lambda i, bits: (0, 0, 0)) for x in keep]
    others = [(x, (1, r, wide), lambda i, bits: (0, 0, 0)) for x in got]
    have = plain_call(
        add_blocks, core, 1, ones + others, [((1, r, wide), (1, r, wide), lambda i, bits: (0, 0, 0))] * PARTS, "add_blocks"
    )
    for k, level in enumerate(reversed(levels)):
        got = [flip(x, *link) for x, link in zip(have, level)]
        ins = [(x, (n, r, wide), lambda i, bits: (0, 0, 0)) for x in (*have, *got)]
        outs = [((2 * n, r, wide), (n, r, wide), lambda i, bits: (i, 0, 0))] * PARTS
        have = plain_call(merge_blocks, level_bits(level), 2, ins, outs, "merge_blocks")
        n *= 2
    whole = jnp.stack(have)
    other = flip(whole, "head", 1)
    whole, other = (x.reshape(PARTS * part_rows, wide) for x in (whole, other))
    return plain_call(
        unpack_blocks,
        core,
        2,
        [(x, (PARTS * part_rows, wide), lambda i, core: (0, 0)) for x in (whole, other)],
        [((rows, w), (rows // 2, w), lambda i, core: (i, 0)) for w in widths],
        "unpack_blocks",
    )


def positions(patches, count):
    slots = patches.shape[1]
    live = jnp.arange(slots, dtype=jnp.int32)[None, :] < count[:, None]
    row = jnp.where(live, (patches // GRID).astype(F32), FAR)
    column = (patches % GRID).astype(F32)
    pos = jnp.stack((row, column), axis=1)
    return jnp.pad(pos, ((0, 0), (0, 0), (0, 256 - slots)), constant_values=FAR)


def flip(values, axis_name, bit):
    size = lax.axis_size(axis_name)
    return lax.ppermute(values, axis_name, [(i, i ^ bit) for i in range(size)])


def gather_group(values, after):
    size = lax.axis_size("head")
    reach = {0: values}
    bit = size // 2
    while bit:
        sent = dict(reach)
        for r in sent:
            if r:
                sent[r], after = lax.optimization_barrier((sent[r], after))
            reach[r ^ bit] = flip(sent[r], "head", bit)
        bit //= 2
    return [reach[r] for r in range(size)], after


def row_product(left, right):
    return lax.dot_general(
        left.reshape(-1, left.shape[-1]),
        right.reshape(-1, right.shape[-1]),
        (((0,), (0,)), ((), ())),
        preferred_element_type=F32,
    )


def total(values):
    return lax.psum(values, ("dp", "head"))


def body(
    radar, optical, cotangent, radar_ratio, optical_ratio, radar_patches, optical_patches, pairing,
    norm_gain, norm_bias, self_qkv, self_out, cross_q, cross_kv, cross_out,
    mlp_in, mlp_in_bias, mlp_out, mlp_out_bias,
):
    images, slots, width = radar.shape
    hidden = mlp_in.shape[1]
    me = lax.axis_index("head")
    start = me * images
    gains, shifts = norm_gain.astype(F32), norm_bias.astype(F32)

    def own(values):
        return lax.dynamic_slice_in_dim(values, start, images, 0)


    radar_count = GRID * GRID * (100 - own(radar_ratio)) // 100
    partner = own(pairing)
    other_count = (GRID * GRID * (100 - optical_ratio) // 100)[partner]
    pos = positions(own(radar_patches), radar_count)
    other_pos = positions(optical_patches[partner], other_count)

    rows = images * slots
    wide_p = HEADS * 256 if slots > 128 else HEADS * slots
    attention = 2 * images * HEADS * slots * 256 * HEAD_DIM
    h1, qkv, p1, o1, x1, h2, q2 = images_call(
        self_forward,
        (radar_count,),
        (radar, pos),
        (gains, shifts, self_qkv, self_out, cross_q),
        [
            ((slots, width), BF16),
            ((slots, 3 * width), BF16),
            ((slots, wide_p), BF16),
            ((slots, width), BF16),
            ((slots, width), F32),
            ((slots, width), BF16),
            ((slots, width), BF16),
        ],
        [],
        [],
        2 * rows * width * width * 5 + 2 * attention,
        "self_forward",
    )
    optical_blocks, x1 = gather_group(optical, x1)
    paired = take_call(partner // images ^ me, partner % images, optical_blocks)
    mixed, kv, p2, o2, h3, g, du, dm, dx2, sums3, in_sums = images_call(
        cross_and_mlp,
        (radar_count, other_count),
        (x1, q2, paired, cotangent, pos, other_pos),
        (
            gains, shifts, cross_kv, cross_out, mlp_in, mlp_in_bias.astype(F32)[None],
            mlp_out, mlp_out_bias.astype(F32)[None],
        ),
        [
            ((slots, width), BF16),
            ((slots, 2 * width), BF16),
            ((slots, wide_p), BF16),
            ((slots, width), BF16),
            ((slots, width), BF16),
            ((slots, hidden), BF16),
            ((slots, hidden), BF16),
            ((slots, width), BF16),
            ((slots, width), F32),
        ],
        [(3, width), (1, hidden)],
        [],
        2 * rows * width * (3 * width + 4 * hidden) + 2 * attention,
        "cross_and_mlp",
    )
    grad_mlp_out, grad_mlp_in = row_product(g, dm).astype(BF16), row_product(h3, du).astype(BF16)
    grad_mlp_out, grad_mlp_in, dx2 = lax.optimization_barrier((grad_mlp_out, grad_mlp_in, dx2))
    grad_mlp_out, grad_mlp_in = total((grad_mlp_out, grad_mlp_in))
    da2, dq2, dkv, og, dx1, sums2 = images_call(
        cross_back,
        (other_count,),
        (dx2, x1, q2, kv, p2),
        (gains, cross_out, cross_q, cross_kv),
        [
            ((slots, width), BF16),
            ((slots, width), BF16),
            ((slots, 2 * width), BF16),
            ((slots, width), BF16),
            ((slots, width), F32),
        ],
        [(2, width)],
        [((slots, width), BF16)],
        2 * rows * width * width * 4 + 4 * attention,
        "cross_back",
    )
    first_group = (
        row_product(o2, da2).astype(BF16),
        row_product(h2, dq2).astype(BF16),
        row_product(paired, dkv).astype(BF16),
        row_product(o1, dx1.astype(BF16)).astype(BF16),
    )
    first_group, dx1 = lax.optimization_barrier((first_group, dx1))
    grad_cross_out, grad_cross_q, grad_cross_kv, grad_self_out = total_by_halves(first_group)
    dqkv, radar_grad, sums1 = images_call(
        self_back,
        (radar_count,),
        (dx1, radar, qkv, p1),
        (gains, self_out, self_qkv),
        [((slots, 3 * width), BF16), ((slots, width), BF16)],
        [(2, width)],
        [((slots, width), BF16)],
        2 * rows * width * width * 4 + 4 * attention,
        "self_back",
    )
    og_blocks, dqkv = gather_group(og, dqkv)
    inverse_pairing = own(jnp.argsort(pairing))
    optical_grad = take_call(inverse_pairing // images ^ me, inverse_pairing % images, og_blocks)
    grad_self_qkv = row_product(h1, dqkv).astype(BF16)
    small = jnp.concatenate((sums1, sums2, sums3, in_sums.reshape(-1, width)), axis=0)
    count = small.shape[0]
    small = jnp.pad(small.astype(BF16).T, ((0, 0), (0, 128 - count)))
    grad_self_qkv, small = total_by_halves((grad_self_qkv, small))
    small = small[:, :count].T
    gain_grads = jnp.stack((small[0], small[2], small[4]))
    shift_grads = jnp.stack((small[1], small[3], small[5]))
    grad_mlp_in_bias, grad_mlp_out_bias = small[7:].reshape(hidden), small[6]
    return (
        mixed, radar_grad, optical_grad, gain_grads.astype(BF16), shift_grads.astype(BF16),
        grad_self_qkv, grad_self_out, grad_cross_q, grad_cross_kv, grad_cross_out,
        grad_mlp_in, grad_mlp_in_bias.astype(BF16), grad_mlp_out, grad_mlp_out_bias.astype(BF16),
    )


def solution(mesh):
    split, group, copied = P(("dp", "head"), None, None), P("dp"), P()
    return jax.shard_map(
        body,
        mesh=mesh,
        in_specs=(split,) * 3 + (group,) * 5 + (copied,) * 11,
        out_specs=(split,) * 3 + (copied,) * 11,
        check_vma=False,
    )
```

```python
from functools import partial
import math

import jax
import jax.numpy as jnp
from jax import lax
from jax.experimental import pallas as pl
from jax.experimental.pallas import tpu as pltpu
from jax.sharding import PartitionSpec as P

HEADS = 12
HEAD_DIM = 64
GRID = 15
PAIR = 2
QUAD = 4
WIDE = QUAD * HEAD_DIM
FAR = 1e15
VMEM_BYTES = 61 * 1024 * 1024
SLOPES = [2.0 ** (-8.0 * (h + 1.0) / HEADS) for h in range(HEADS)]
SCALE = 1.0 / math.sqrt(HEAD_DIM)
F32 = jnp.float32
BF16 = jnp.bfloat16
SMALL_COST = pl.CostEstimate(flops=1, bytes_accessed=1, transcendentals=0)


def mm(left, right):
    return jnp.dot(left, right, preferred_element_type=F32)


def mm_t(left, right):
    return lax.dot_general(left, right, (((1,), (1,)), ((), ())), preferred_element_type=F32)


def t_mm(left, right):
    return lax.dot_general(left, right, (((0,), (0,)), ((), ())), preferred_element_type=F32)


def rows_of(ref):
    value = ref[...].astype(F32)
    return value.reshape(value.shape[0] * value.shape[1], value.shape[2])


def put_rows(ref, value):
    slots = ref.shape[1]
    for i in range(ref.shape[0]):
        ref[i] = value[i * slots : (i + 1) * slots].astype(ref.dtype)


def norm(values):
    centre = values - jnp.mean(values, axis=-1, keepdims=True)
    inverse = lax.rsqrt(jnp.mean(centre * centre, axis=-1, keepdims=True) + 1e-6)
    return centre * inverse, inverse


def norm_back(grad, scaled, inverse, gain):
    weighted = grad * gain
    return inverse * (
        weighted
        - jnp.mean(weighted, axis=-1, keepdims=True)
        - scaled * jnp.mean(weighted * scaled, axis=-1, keepdims=True)
    )


def column_sum(values):
    return jnp.sum(values, axis=0, keepdims=True)


def head_masks(dtype):
    lane = lax.broadcasted_iota(jnp.int32, (1, WIDE), 1) // HEAD_DIM
    return [(lane == h).astype(F32).astype(dtype) for h in range(QUAD)]


def as_column(row, slots):
    n = row.shape[1]
    same = lax.broadcasted_iota(jnp.int32, (slots, n), 0) == lax.broadcasted_iota(
        jnp.int32, (slots, n), 1
    )
    return jnp.sum(jnp.where(same, jnp.broadcast_to(row, (slots, n)), 0.0), axis=1, keepdims=True)


def distances(query_pos, key_pos, slots, keys):
    delta_row = as_column(query_pos[0:1], slots) - key_pos[0:1, :keys]
    delta_column = as_column(query_pos[1:2], slots) - key_pos[1:2, :keys]
    return jnp.sqrt(delta_row * delta_row + delta_column * delta_column)


def stacked(block, keys, masks):
    slots = block.shape[0]
    if keys <= slots:
        part = block[:keys]
    else:
        part = jnp.concatenate(
            (block.astype(F32), jnp.zeros((keys - slots, block.shape[1]), F32)), axis=0
        ).astype(BF16)
    return jnp.concatenate([part * m for m in masks], axis=0)


def attend(i, keys, q_of, k_of, v_of, query_pos, key_pos, p_ref, o_ref):
    slots = o_ref.shape[1]
    dist = distances(query_pos, key_pos, slots, keys)
    masks = head_masks(BF16)
    for g in range(HEADS // QUAD):
        q = q_of(g) * jnp.asarray(SCALE, BF16)
        scores = mm_t(q, stacked(k_of(g), keys, masks))
        parts = []
        for h in range(QUAD):
            s = scores[:, h * keys : (h + 1) * keys] - SLOPES[g * QUAD + h] * dist
            e = jnp.exp(s - jnp.max(s, axis=1, keepdims=True))
            parts.append((e * (1.0 / jnp.sum(e, axis=1, keepdims=True))).astype(BF16))
        p = jnp.concatenate(parts, axis=1)
        p_ref[i, :, g * QUAD * keys : (g + 1) * QUAD * keys] = p
        o_ref[i, :, g * WIDE : (g + 1) * WIDE] = mm(p, stacked(v_of(g), keys, masks)).astype(BF16)


def attend_back(i, keys, q_of, k_of, v_of, do_of, p_ref, put_dq, put_dk, put_dv, slots):
    masks = head_masks(BF16)
    wide_masks = head_masks(F32)

    def gathered(product):
        total = sum(product[h * keys : (h + 1) * keys] * wide_masks[h] for h in range(QUAD))
        if keys >= slots:
            return total[:slots]
        return jnp.concatenate((total, jnp.zeros((slots - keys, WIDE), F32)), axis=0)

    for g in range(HEADS // QUAD):
        q, do = q_of(g), do_of(g)
        keys_stack = stacked(k_of(g), keys, masks)
        dp = mm_t(do, stacked(v_of(g), keys, masks))
        p = p_ref[i, :, g * QUAD * keys : (g + 1) * QUAD * keys]
        parts = []
        for h in range(QUAD):
            ph = p[:, h * keys : (h + 1) * keys].astype(F32)
            t = ph * dp[:, h * keys : (h + 1) * keys]
            parts.append((t - ph * jnp.sum(t, axis=1, keepdims=True)).astype(BF16))
        ds = jnp.concatenate(parts, axis=1)
        put_dv(g, gathered(t_mm(p, do)).astype(BF16))
        put_dq(g, (mm(ds, keys_stack) * SCALE).astype(BF16))
        put_dk(g, (gathered(t_mm(ds, q)) * SCALE).astype(BF16))


def by_count(count, slots, work):
    small = min(slots, 128)
    pl.when(count <= small)(lambda: work(small))
    if slots > small:
        pl.when(count > small)(lambda: work(256))


def gelu_parts(u):
    size = jnp.abs(u)
    t = 1.0 / (1.0 + (0.3275911 / math.sqrt(2.0)) * size)
    poly = 0.5 * 1.061405429
    for c in (-1.453152027, 1.421413741, -0.284496736, 0.254829592):
        poly = poly * t + 0.5 * c
    bell = jnp.exp(-0.5 * (u * u))
    tail = poly * t * bell
    phi_cap = jnp.where(u >= 0.0, 1.0 - tail, tail)
    return u * phi_cap, phi_cap + u * (bell * (1.0 / math.sqrt(2.0 * math.pi)))


def live_rows(counts, slots):
    slot = lax.broadcasted_iota(jnp.int32, (slots, 1), 0)
    return jnp.concatenate([(slot < c).astype(F32) for c in counts], axis=0)


def self_forward(
    base, count, x_ref, pos_ref, gain_ref, shift_ref, qkv_w, out_w, q_w,
    h1_ref, qkv_ref, p_ref, o_ref, x1_ref, h2_ref, q2_ref,
):
    step = pl.program_id(0)
    pair, slots, width = x_ref.shape
    x = rows_of(x_ref)
    scaled, _ = norm(x)
    h1 = (scaled * gain_ref[...].astype(F32)[0:1] + shift_ref[...].astype(F32)[0:1]).astype(BF16)
    put_rows(h1_ref, h1.astype(F32))
    put_rows(qkv_ref, mm(h1, qkv_w[...]))
    for i in range(pair):

        def block(kind, i=i):
            return lambda g: qkv_ref[i, :, kind * width + g * WIDE : kind * width + (g + 1) * WIDE]

        by_count(
            count[base + step * pair + i],
            slots,
            lambda keys, i=i, block=block: attend(
                i, keys, block(0), block(1), block(2), pos_ref[i], pos_ref[i], p_ref, o_ref
            ),
        )
    x1 = x + mm(rows_of(o_ref).astype(BF16), out_w[...])
    put_rows(x1_ref, x1)
    scaled, _ = norm(x1)
    h2 = (scaled * gain_ref[...].astype(F32)[1:2] + shift_ref[...].astype(F32)[1:2]).astype(BF16)
    put_rows(h2_ref, h2.astype(F32))
    put_rows(q2_ref, mm(h2, q_w[...]))


def cross_and_mlp(
    base, count, other_count, x1_ref, q2_ref, opt_ref, dy_ref, pos_ref, other_pos_ref, gain_ref, shift_ref,
    kv_w, out_w, in_w, in_b, mo_w, mo_b,
    mixed_ref, kv_ref, p_ref, o_ref, h3_ref, g_ref, du_ref, dm_ref, dx2_ref, sums_ref, in_sums_ref,
):
    step = pl.program_id(0)
    pair, slots, width = x1_ref.shape
    hidden = in_w.shape[1]
    put_rows(kv_ref, mm(rows_of(opt_ref).astype(BF16), kv_w[...]))
    for i in range(pair):

        def block(ref, kind, i=i):
            return lambda g: ref[i, :, kind * width + g * WIDE : kind * width + (g + 1) * WIDE]

        by_count(
            other_count[base + step * pair + i],
            slots,
            lambda keys, i=i, block=block: attend(
                i, keys, block(q2_ref, 0), block(kv_ref, 0), block(kv_ref, 1),
                pos_ref[i], other_pos_ref[i], p_ref, o_ref,
            ),
        )
    x2 = rows_of(x1_ref) + mm(rows_of(o_ref).astype(BF16), out_w[...])
    scaled, inverse = norm(x2)
    gain = gain_ref[...].astype(F32)[2:3]
    h3 = (scaled * gain + shift_ref[...].astype(F32)[2:3]).astype(BF16)
    put_rows(h3_ref, h3.astype(F32))
    live = live_rows([count[base + step * pair + i] for i in range(pair)], slots)
    dy = rows_of(dy_ref) * live
    dm = dy.astype(BF16)
    put_rows(dm_ref, dy)
    chunk = 768
    g_parts, du_parts, in_sums = [], [], []
    for j in range(hidden // chunk):
        cols = slice(j * chunk, (j + 1) * chunk)
        u = mm(h3, in_w[:, cols]) + in_b[0:1, cols]
        dg = mm_t(dm, mo_w[cols, :]).astype(BF16).astype(F32)
        g, slope = gelu_parts(u)
        du = dg * slope
        for i in range(pair):
            rows = slice(i * slots, (i + 1) * slots)
            g_ref[i, :, cols] = g[rows].astype(BF16)
            du_ref[i, :, cols] = du[rows].astype(BF16)
        g_parts.append(g.astype(BF16))
        du_parts.append(du.astype(BF16))
        in_sums.append(column_sum(du.astype(BF16).astype(F32)))
    y = x2 + (mm(jnp.concatenate(g_parts, axis=1), mo_w[...]) + mo_b[0:1])
    put_rows(mixed_ref, y * live)
    dh3 = mm_t(jnp.concatenate(du_parts, axis=1), in_w[...])
    put_rows(dx2_ref, dy + norm_back(dh3, scaled, inverse, gain))
    sums = jnp.concatenate((column_sum(dh3 * scaled), column_sum(dh3), column_sum(dy)), axis=0)
    in_sums = jnp.concatenate(in_sums, axis=1)

    @pl.when(step == 0)
    def _():
        sums_ref[...] = sums
        in_sums_ref[...] = in_sums

    @pl.when(step > 0)
    def _():
        sums_ref[...] += sums
        in_sums_ref[...] += in_sums


def cross_back(
    base, other_count, dx2_ref, x1_ref, q2_ref, kv_ref, p_ref, gain_ref, out_w, q_w, kv_w,
    da2_ref, dq2_ref, dkv_ref, og_ref, dx1_ref, sums_ref, do_ref,
):
    step = pl.program_id(0)
    pair, slots, width = x1_ref.shape
    dx2 = rows_of(dx2_ref)
    da2 = dx2.astype(BF16)
    put_rows(da2_ref, dx2)
    put_rows(do_ref, mm_t(da2, out_w[...]))
    for i in range(pair):

        def block(ref, kind, i=i):
            return lambda g: ref[i, :, kind * width + g * WIDE : kind * width + (g + 1) * WIDE]

        def put(ref, kind, i=i):
            def store(g, value):
                ref[i, :, kind * width + g * WIDE : kind * width + (g + 1) * WIDE] = value

            return store

        by_count(
            other_count[base + step * pair + i],
            slots,
            lambda keys, i=i, block=block, put=put: attend_back(
                i, keys, block(q2_ref, 0), block(kv_ref, 0), block(kv_ref, 1), block(do_ref, 0),
                p_ref, put(dq2_ref, 0), put(dkv_ref, 0), put(dkv_ref, 1), slots,
            ),
        )
    put_rows(og_ref, mm_t(rows_of(dkv_ref).astype(BF16), kv_w[...]))
    dh2 = mm_t(rows_of(dq2_ref).astype(BF16), q_w[...])
    scaled, inverse = norm(rows_of(x1_ref))
    put_rows(dx1_ref, dx2 + norm_back(dh2, scaled, inverse, gain_ref[...].astype(F32)[1:2]))
    sums = jnp.concatenate((column_sum(dh2 * scaled), column_sum(dh2)), axis=0)

    @pl.when(step == 0)
    def _():
        sums_ref[...] = sums

    @pl.when(step > 0)
    def _():
        sums_ref[...] += sums


def self_back(
    base, count, dx1_ref, x_ref, qkv_ref, p_ref, gain_ref, out_w, qkv_w,
    dqkv_ref, dx_ref, sums_ref, do_ref,
):
    step = pl.program_id(0)
    pair, slots, width = x_ref.shape
    dx1 = rows_of(dx1_ref)
    da1 = dx1.astype(BF16)
    put_rows(do_ref, mm_t(da1, out_w[...]))
    for i in range(pair):

        def block(ref, kind, i=i):
            return lambda g: ref[i, :, kind * width + g * WIDE : kind * width + (g + 1) * WIDE]

        def put(ref, kind, i=i):
            def store(g, value):
                ref[i, :, kind * width + g * WIDE : kind * width + (g + 1) * WIDE] = value

            return store

        by_count(
            count[base + step * pair + i],
            slots,
            lambda keys, i=i, block=block, put=put: attend_back(
                i, keys, block(qkv_ref, 0), block(qkv_ref, 1), block(qkv_ref, 2), block(do_ref, 0),
                p_ref, put(dqkv_ref, 0), put(dqkv_ref, 1), put(dqkv_ref, 2), slots,
            ),
        )
    dh1 = mm_t(rows_of(dqkv_ref).astype(BF16), qkv_w[...])
    scaled, inverse = norm(rows_of(x_ref))
    put_rows(dx_ref, dx1 + norm_back(dh1, scaled, inverse, gain_ref[...].astype(F32)[0:1]))
    sums = jnp.concatenate((column_sum(dh1 * scaled), column_sum(dh1)), axis=0)

    @pl.when(step == 0)
    def _():
        sums_ref[...] = sums

    @pl.when(step > 0)
    def _():
        sums_ref[...] += sums


def take_images(source, place, *refs):
    j = pl.program_id(0)
    for r, ref in enumerate(refs[:-1]):

        @pl.when(source[j] == r)
        def _(ref=ref):
            refs[-1][...] = ref[...]


def split_first(core, bits, *refs):
    outs = refs[-2 * PARTS :]
    count = (len(refs) - 2 * PARTS) // (4 * PARTS)
    for place, out in enumerate(outs):
        column = 0
        for k in range(count):
            first = (place * count + k) * 2
            value = refs[first][...].astype(F32) + refs[first + 1][...].astype(F32)
            chunk, r, _ = out.shape
            for j in range(chunk):
                out[j, :, column : column + value.shape[1]] = value[j * r : (j + 1) * r].astype(out.dtype)
            column += value.shape[1]


def add_blocks(bits, *refs):
    third = len(refs) // 3
    for one, other, out in zip(refs[:third], refs[third : 2 * third], refs[2 * third :]):
        out[...] = (one[...].astype(F32) + other[...].astype(F32)).astype(out.dtype)


def unpack_blocks(core, bits, *refs):
    outs = refs[4 * PARTS :]
    here = pl.program_id(0) == core[0]

    for p in range(PARTS):
        own = pl.program_id(1) == bits[p]
        for where, first in ((here, 0), (jnp.logical_not(here), 2)):
            for whose, second in ((own, 0), (jnp.logical_not(own), 1)):

                @pl.when(jnp.logical_and(where, whose))
                def _(source=refs[(first + second) * PARTS + p], p=p):
                    column = 0
                    for out in outs:
                        out[0, p, 0] = source[:, :, column : column + out.shape[-1]]
                        column += out.shape[-1]


def merge_blocks(bits, *refs):
    third = len(refs) // 3
    half = pl.program_id(0)
    for p, (one, other, out) in enumerate(zip(refs[:third], refs[third : 2 * third], refs[2 * third :])):

        @pl.when(half == bits[p])
        def _(one=one, out=out):
            out[...] = one[...].reshape(out.shape)

        @pl.when(half != bits[p])
        def _(other=other, out=out):
            out[...] = other[...].reshape(out.shape)


class Thread:
    def __init__(self, arrays):
        self.arrays = tuple(arrays)


def passing(after):
    threads = [x for x in after if isinstance(x, Thread)]
    waits = [x for x in after if not isinstance(x, Thread)]
    through = [x for t in threads for x in t.arrays]

    def hand_back(results):
        results = list(results)
        for t in threads:
            t.arrays, results = tuple(results[: len(t.arrays)]), results[len(t.arrays) :]

    return waits, through, hand_back


def images_call(kernel, scalars, arrays, whole, outs, sums, scratch, flops, name, part=(0, 1), into=None, after=()):
    images = arrays[0].shape[0]
    pair = PAIR if images % PAIR == 0 else 1
    steps = images // pair // part[1]
    first = part[0] * steps
    into = into or ()

    def split_spec(shape):
        rank = len(shape)
        return pl.BlockSpec((pair,) + tuple(shape[1:]), lambda i, *s: (i + first,) + (0,) * (rank - 1))

    def whole_spec(shape):
        rank = len(shape)
        return pl.BlockSpec(tuple(shape), lambda i, *s: (0,) * rank, pipeline_mode=pl.Buffered(1))

    out_shapes = [jax.ShapeDtypeStruct((images,) + tail, dtype) for tail, dtype in outs]
    sum_shapes = [jax.ShapeDtypeStruct(shape, F32) for shape in sums]
    waits, through, hand_back = passing(after)
    free = [*waits, *into, *through]
    n_used = len(scalars) + len(arrays) + len(whole)
    n_outs = len(out_shapes) + len(sum_shapes)
    shapes = out_shapes + sum_shapes + [jax.ShapeDtypeStruct(x.shape, x.dtype) for x in through]

    def run(*refs):
        refs, rest = refs[:n_used], refs[n_used + len(free) :]
        kernel(first * pair, *refs, *rest[:n_outs], *rest[n_outs + len(through) :])

    aliases = {n_used + len(waits) + k: k for k in range(len(into))}
    aliases |= {n_used + len(waits) + len(into) + k: n_outs + k for k in range(len(through))}
    results = pl.pallas_call(
        run,
        grid_spec=pltpu.PrefetchScalarGridSpec(
            num_scalar_prefetch=len(scalars),
            grid=(steps,),
            in_specs=[split_spec(a.shape) for a in arrays]
            + [whole_spec(a.shape) for a in whole]
            + [pl.BlockSpec(memory_space=pl.ANY)] * len(free),
            out_specs=[split_spec(o.shape) for o in out_shapes]
            + [pl.BlockSpec(s.shape, lambda i, *_: (0, 0)) for s in sum_shapes]
            + [pl.BlockSpec(memory_space=pl.ANY)] * len(through),
            scratch_shapes=[pltpu.VMEM((pair,) + tail, dtype) for tail, dtype in scratch],
        ),
        out_shape=shapes,
        input_output_aliases=aliases,
        compiler_params=pltpu.CompilerParams(vmem_limit_bytes=VMEM_BYTES),
        cost_estimate=SMALL_COST,
        name=name,
    )(*scalars, *arrays, *whole, *free)
    hand_back(results[n_outs:])
    return results[:n_outs]


def take_call(source, place, sources):
    shape = sources[0].shape
    block = (1,) + shape[1:]

    def spec(r):
        return pl.BlockSpec(block, lambda j, source, place: (jnp.where(source[j] == r, place[j], 0), 0, 0))

    return pl.pallas_call(
        take_images,
        grid_spec=pltpu.PrefetchScalarGridSpec(
            num_scalar_prefetch=2,
            grid=(shape[0],),
            in_specs=[spec(r) for r in range(len(sources))],
            out_specs=pl.BlockSpec(block, lambda j, source, place: (j, 0, 0)),
        ),
        out_shape=jax.ShapeDtypeStruct(shape, sources[0].dtype),
        cost_estimate=SMALL_COST,
        name="take_images",
    )(source, place, *sources)


def plain_call(kernel, scalars, grid, ins, outs, name, after=()):
    waits, through, hand_back = passing(after)
    free = [*waits, *through]
    n_used, n_outs = len(scalars) + len(ins), len(outs)

    def run(*refs):
        refs, rest = refs[:n_used], refs[n_used + len(free) :]
        kernel(*refs, *rest[:n_outs])

    results = pl.pallas_call(
        run,
        grid_spec=pltpu.PrefetchScalarGridSpec(
            num_scalar_prefetch=len(scalars),
            grid=grid,
            in_specs=[pl.BlockSpec(block, index) for _, block, index in ins]
            + [pl.BlockSpec(memory_space=pl.ANY)] * len(free),
            out_specs=[pl.BlockSpec(block, index) for _, block, index in outs]
            + [pl.BlockSpec(memory_space=pl.ANY)] * len(through),
        ),
        out_shape=[jax.ShapeDtypeStruct(shape, BF16) for shape, _, _ in outs]
        + [jax.ShapeDtypeStruct(x.shape, x.dtype) for x in through],
        input_output_aliases={n_used + len(waits) + k: n_outs + k for k in range(len(through))},
        compiler_params=pltpu.CompilerParams(vmem_limit_bytes=VMEM_BYTES),
        cost_estimate=SMALL_COST,
        name=name,
    )(*scalars, *[a for a, _, _ in ins], *free)
    hand_back(results[n_outs:])
    return results[:n_outs]


def bit_of(axis_name, bit):
    return (lax.axis_index(axis_name) // bit) % 2


def own_place():
    return lax.axis_index("chip") * 2 + lax.axis_index("core")


PARTS = 3


def sum_links(turn):
    chip, dp = lax.axis_size("chip"), lax.axis_size("dp")
    links = [("chip", 2**i) for i in reversed(range(chip.bit_length() - 1))]
    links += [("dp", 2**i) for i in range(dp.bit_length() - 1)]
    return links[turn:PARTS] + links[:turn] + links[PARTS:]


def sum_levels():
    orders = [sum_links(p) for p in range(PARTS)]
    return [list(level) for level in zip(*orders)]


def take_own(refs_every, *outs):
    one, two = outs
    for j in range(refs_every.shape[0]):
        r = refs_every.shape[2]
        one[j] = refs_every[j, 0]
        wide = two.shape[3]
        for k in range(two.shape[1]):
            two[j, k] = refs_every[j, 1, :, k * wide : (k + 1) * wide]


def total_of_pieces(products):
    core = bit_of("core", 1)
    orders = [sum_links(0)[k:] + sum_links(0)[:k] for k in range(len(products))]
    chip, dp = lax.axis_size("chip").bit_length() - 1, lax.axis_size("dp").bit_length() - 1
    links = [("dp", 2**i) for i in reversed(range(dp))] + [("chip", 2**i) for i in reversed(range(chip))]
    got = [flip(product(1 - core).astype(BF16), "core", 1) for product in products]
    keep, shapes = [], []
    for product, more in zip(products, got):
        kept = (product(core) + more.astype(F32)).astype(BF16)
        shapes.append((2 * kept.shape[0], kept.shape[1]))
        keep.append(kept.reshape((2,) * len(links) + (kept.shape[0] // 2 ** len(links), kept.shape[1])))
    for k in range(len(links)):
        send = []
        for m, order in enumerate(orders):
            b, axis = bit_of(*order[k]), links.index(order[k])
            send.append(lax.dynamic_slice_in_dim(keep[m], 1 - b, 1, axis))
            keep[m] = lax.dynamic_slice_in_dim(keep[m], b, 1, axis)
        got = [flip(x, *order[k]) for x, order in zip(send, orders)]
        keep = yield tuple(send) + (Thread(keep),)
        keep = [(one.astype(F32) + more.astype(F32)).astype(BF16) for one, more in zip(keep, got)]
    (r, wide), (rows, columns) = sorted(x.shape[-2:] for x in keep)
    parts = rows // r
    pieces = []
    for x in keep:
        x = x.reshape(-1, r, x.shape[-1])
        pieces.append(x.swapaxes(0, 1).reshape(1, r, wide))
    pieces = jnp.stack(pieces, axis=1)
    every = lax.all_gather(pieces, ("core", "dp", "chip"), axis=0, tiled=True)
    yield (pieces,)
    count = every.shape[0]
    chunk = 4
    tall = [m for m, x in enumerate(keep) if x.shape[-2] != r]
    tall = tall[0] if tall else 1
    one, two = pl.pallas_call(
        take_own,
        grid=(count // chunk,),
        in_specs=[pl.BlockSpec((chunk, 2, r, wide), lambda i: (i, 0, 0, 0))],
        out_specs=[
            pl.BlockSpec((chunk, r, wide), lambda i: (i, 0, 0)),
            pl.BlockSpec((chunk, parts, r, columns), lambda i: (i, 0, 0, 0)),
        ],
        out_shape=[
            jax.ShapeDtypeStruct((count, r, wide), BF16),
            jax.ShapeDtypeStruct((count, parts, r, columns), BF16),
        ],
        compiler_params=pltpu.CompilerParams(vmem_limit_bytes=VMEM_BYTES),
        cost_estimate=SMALL_COST,
        name="take_own",
    )(every)
    yield [one.reshape(shapes[0]), two.reshape(shapes[1])]


def exchange(arrays, level):
    if len(set(level)) == 1:
        got = flip(jnp.concatenate(arrays, axis=0), *level[0])
        return [(got, p * arrays[0].shape[0]) for p in range(len(arrays))]
    return [(flip(x, *link), 0) for x, link in zip(arrays, level)]


def total_by_halves(products):
    levels = sum_levels()
    core = bit_of("core", 1)

    def scalars(level):
        return jnp.stack([bit_of(*link) for link in level]).astype(jnp.int32)

    got = [flip(product(1 - core).astype(BF16), "core", 1) for product in products]
    keep = [product(core).astype(BF16) for product in products]
    after = yield (keep[0],)
    rows = 2 * keep[0].shape[0]
    widths = [m.shape[1] for m in keep]
    wide = sum(widths)
    n = 2 ** len(levels)
    r = rows // (2 * PARTS * n)
    half = n // 2
    chunk = min(half, max(1, 16 // r))
    core = core[None].astype(jnp.int32)
    ins = []
    for other in (True, False):
        for p in range(PARTS):
            for one, more in zip(keep, got):

                def index(i, core, bits, p=p, other=other):
                    b = 1 - bits[p] if other else bits[p]
                    return ((p * n + b * half) // chunk + i, 0)

                ins += [(x, (chunk * r, x.shape[1]), index) for x in (one, more)]
    outs = [((half, r, wide), (chunk, r, wide), lambda i, core, bits: (i, 0, 0))] * (2 * PARTS)
    done = plain_call(split_first, (core, scalars(levels[0])), (half // chunk,), ins, outs, "split_first", after)
    for k, level in enumerate(levels):
        send, keep = done[:PARTS], done[PARTS:]
        got = exchange(send, level)
        after = yield (keep[0],)
        n //= 2
        if k + 1 == len(levels):
            break
        half = n // 2
        chunk = min(half, max(1, 16 // r))
        ones, others = [], []
        for other in (True, False):
            for p in range(PARTS):

                def index(i, bits, p=p, other=other, first=0):
                    b = 1 - bits[p] if other else bits[p]
                    return ((first + b * half) // chunk + i, 0, 0)

                ones.append((keep[p], (chunk, r, wide), index))
                others.append((got[p][0], (chunk, r, wide), partial(index, first=got[p][1])))
        outs = [((half, r, wide), (chunk, r, wide), lambda i, bits: (i, 0, 0))] * (2 * PARTS)
        done = plain_call(add_blocks, (scalars(levels[k + 1]),), (half // chunk,), ones + others, outs, "add_blocks", after)
    ins = [(x, (1, r, wide), lambda i, bits, f=f: (f, 0, 0)) for x, f in [(x, 0) for x in keep] + got]
    have = plain_call(
        add_blocks, (core,), (1,), ins, [((1, r, wide), (1, r, wide), lambda i, bits: (0, 0, 0))] * PARTS, "add_blocks", after
    )
    for level in reversed(levels):
        got = exchange(have, level)
        if level is levels[0]:
            got = [x for x, _ in got]
            break
        after = yield (have[0],)
        ins = [(x, (n, r, wide), lambda i, bits, f=f // n: (f, 0, 0)) for x, f in [(x, 0) for x in have] + got]
        outs = [((2 * n, r, wide), (n, r, wide), lambda i, bits: (i, 0, 0))] * PARTS
        have = plain_call(merge_blocks, (scalars(level),), (2,), ins, outs, "merge_blocks", after)
        n *= 2
    other_have = [flip(x, "core", 1) for x in have]
    other_got = [flip(x, "core", 1) for x in got]
    after = yield (have[0],)
    sums = plain_call(
        unpack_blocks,
        (core, scalars(levels[0])),
        (2, 2),
        [(x, (n, r, wide), lambda h, b, core, bits: (0, 0, 0)) for x in (*have, *got, *other_have, *other_got)],
        [((2, PARTS, 2, n, r, w), (1, PARTS, 1, n, r, w), lambda h, b, core, bits: (h, 0, b, 0, 0, 0)) for w in widths],
        "unpack_blocks",
        after,
    )
    yield [x.reshape(rows, w) for x, w in zip(sums, widths)]


def half_of_rows(left, right):
    def product(half):
        flat = left.reshape(-1, left.shape[-1])
        wide = flat.shape[1] // 2
        return row_product(lax.dynamic_slice_in_dim(flat, half * wide, wide, 1), right)

    return product


def half_of(values):
    rows = values.shape[0] // 2
    return lambda half: lax.dynamic_slice_in_dim(values, half * rows, rows, 0)


def positions(patches, count):
    slots = patches.shape[1]
    live = jnp.arange(slots, dtype=jnp.int32)[None, :] < count[:, None]
    row = jnp.where(live, (patches // GRID).astype(F32), FAR)
    column = (patches % GRID).astype(F32)
    pos = jnp.stack((row, column), axis=1)
    return jnp.pad(pos, ((0, 0), (0, 0), (0, 256 - slots)), constant_values=FAR)


def flip(values, axis_name, bit):
    size = lax.axis_size(axis_name)
    return lax.ppermute(values, axis_name, [(i, i ^ bit) for i in range(size)])


def gather_far(values):
    reach = {0: values}
    bit = lax.axis_size("chip") // 2
    while bit:
        for r in list(reach):
            reach[r ^ (2 * bit)] = flip(reach[r], "chip", bit)
        bit //= 2
    return reach


def gather_near(reach):
    both = {r: x for r, x in reach.items()}
    for r, x in reach.items():
        both[r ^ 1] = flip(x, "core", 1)
    return [both[r] for r in range(len(both))]


def row_product(left, right):
    return lax.dot_general(
        left.reshape(-1, left.shape[-1]),
        right.reshape(-1, right.shape[-1]),
        (((0,), (0,)), ((), ())),
        preferred_element_type=F32,
    )


def total(values):
    return lax.psum(values, ("dp", "chip", "core"))


def body(
    radar, optical, cotangent, radar_ratio, optical_ratio, radar_patches, optical_patches, pairing,
    norm_gain, norm_bias, self_qkv, self_out, cross_q, cross_kv, cross_out,
    mlp_in, mlp_in_bias, mlp_out, mlp_out_bias,
):
    images, slots, width = radar.shape
    hidden = mlp_in.shape[1]
    me = own_place()
    start = me * images
    gains, shifts = norm_gain, norm_bias

    def own(values):
        return lax.dynamic_slice_in_dim(values, start, images, 0)


    radar_count = GRID * GRID * (100 - own(radar_ratio)) // 100
    partner = own(pairing)
    other_count = (GRID * GRID * (100 - optical_ratio) // 100)[partner]
    pos = positions(own(radar_patches), radar_count)
    other_pos = positions(optical_patches[partner], other_count)

    rows = images * slots
    wide_p = HEADS * 256 if slots > 128 else HEADS * slots
    attention = 2 * images * HEADS * slots * 256 * HEAD_DIM
    h1, qkv, p1, o1, x1, h2, q2 = images_call(
        self_forward,
        (radar_count,),
        (radar, pos),
        (gains, shifts, self_qkv, self_out, cross_q),
        [
            ((slots, width), BF16),
            ((slots, 3 * width), BF16),
            ((slots, wide_p), BF16),
            ((slots, width), BF16),
            ((slots, width), F32),
            ((slots, width), BF16),
            ((slots, width), BF16),
        ],
        [],
        [],
        2 * rows * width * width * 5 + 2 * attention,
        "self_forward",
    )
    far, x1 = lax.optimization_barrier((gather_far(optical), x1))
    optical_blocks = gather_near(far)
    paired = take_call(partner // images ^ me, partner % images, optical_blocks)
    mixed, kv, p2, o2, h3, g, du, dm, dx2, sums3, in_sums = images_call(
        cross_and_mlp,
        (radar_count, other_count),
        (x1, q2, paired, cotangent, pos, other_pos),
        (
            gains, shifts, cross_kv, cross_out, mlp_in, mlp_in_bias.astype(F32)[None],
            mlp_out, mlp_out_bias.astype(F32)[None],
        ),
        [
            ((slots, width), BF16),
            ((slots, 2 * width), BF16),
            ((slots, wide_p), BF16),
            ((slots, width), BF16),
            ((slots, width), BF16),
            ((slots, hidden), BF16),
            ((slots, hidden), BF16),
            ((slots, width), BF16),
            ((slots, width), F32),
        ],
        [(3, width), (1, hidden)],
        [],
        2 * rows * width * (3 * width + 4 * hidden) + 2 * attention,
        "cross_and_mlp",
    )
    first = total_of_pieces((half_of_rows(h3, du), half_of_rows(g, dm)))
    before_cross = next(first)
    da2, dq2, dkv, og, dx1, sums2 = images_call(
        cross_back,
        (other_count,),
        (dx2, x1, q2, kv, p2),
        (gains, cross_out, cross_q, cross_kv),
        [
            ((slots, width), BF16),
            ((slots, width), BF16),
            ((slots, 2 * width), BF16),
            ((slots, width), BF16),
            ((slots, width), F32),
        ],
        [(2, width)],
        [((slots, width), BF16)],
        2 * rows * width * width * 4 + 4 * attention,
        "cross_back",
        after=before_cross,
    )
    second = [
        half_of_rows(o2, da2), half_of_rows(h2, dq2), half_of_rows(paired, dkv), half_of_rows(o1, dx1.astype(BF16))
    ]
    core = lax.axis_index("core")
    halves = [tuple(product(half).astype(BF16) for half in (1 - core, core)) for product in second]
    og_far = gather_far(og)

    def step_first(begun):
        return first.send(begun[-1].arrays) if isinstance(begun[-1], Thread) else next(first)

    begun = step_first(before_cross)
    scalars, arrays, whole = (radar_count,), (dx1, radar, qkv, p1), (gains, self_out, self_qkv)
    outs = [((slots, 3 * width), BF16), ((slots, width), BF16)]
    made = None
    for part in range(2):
        *made, sums = images_call(
            self_back, scalars, arrays, whole, outs, [(2, width)], [((slots, width), BF16)], 0, "self_back",
            part=(part, 2), into=made, after=begun + (sum(halves, ()) if part == 0 else ()) + (tuple(og_far[r] for r in og_far if r) if part == 1 else ()),
        )
        sums1 = sums if part == 0 else sums1 + sums
        begun = step_first(begun)
    after = tuple(x for x in begun if not isinstance(x, Thread))
    dqkv, radar_grad = made
    og_blocks = gather_near(og_far)
    inverse_pairing = own(jnp.argsort(pairing))
    optical_grad = take_call(inverse_pairing // images ^ me, inverse_pairing % images, og_blocks)
    small = jnp.concatenate((sums1, sums2, sums3, in_sums.reshape(-1, width)), axis=0)
    count = small.shape[0]
    small = jnp.pad(small.astype(BF16).T, ((0, 0), (0, 128 - count)))
    ready = [iter(pair) for pair in halves]
    second = [lambda half, pair=pair: next(pair) for pair in ready]
    while not isinstance(begun, list):
        begun = step_first(begun)
    grad_mlp_in, grad_mlp_out = begun
    last_round = 2 * len(sum_levels())
    rest = total_by_halves((*second, half_of_rows(h1, dqkv), half_of(small)))
    next(rest)
    rounds = 0
    while not isinstance(after, list):
        rounds += 1
        if rounds == 2:
            after = after + (optical_grad,)
        if rounds == last_round:
            after = after + (grad_mlp_in,)
        after = rest.send(after)
    grad_cross_out, grad_cross_q, grad_cross_kv, grad_self_out, grad_self_qkv, small = after
    small = small[:, :count].T
    gain_grads = jnp.stack((small[0], small[2], small[4]))
    shift_grads = jnp.stack((small[1], small[3], small[5]))
    grad_mlp_in_bias, grad_mlp_out_bias = small[7:].reshape(hidden), small[6]
    return (
        mixed, radar_grad, optical_grad, gain_grads.astype(BF16), shift_grads.astype(BF16),
        grad_self_qkv, grad_self_out, grad_cross_q, grad_cross_kv, grad_cross_out,
        grad_mlp_in, grad_mlp_in_bias.astype(BF16), grad_mlp_out, grad_mlp_out_bias.astype(BF16),
    )


def solution(mesh):
    dp, head = mesh.shape["dp"], mesh.shape["head"]
    mesh = jax.sharding.Mesh(mesh.devices.reshape(dp, head // 2, 2), ("dp", "chip", "core"))
    split, group, copied = P(("dp", "chip", "core"), None, None), P("dp"), P()
    return jax.shard_map(
        body,
        mesh=mesh,
        in_specs=(split,) * 3 + (group,) * 5 + (copied,) * 11,
        out_specs=(split,) * 3 + (copied,) * 11,
        check_vma=False,
    )
```

```python
from functools import partial
import math

import jax
import jax.numpy as jnp
from jax import lax
from jax.experimental import pallas as pl
from jax.experimental.pallas import tpu as pltpu
from jax.sharding import PartitionSpec as P

HEADS = 12
HEAD_DIM = 64
GRID = 15
PAIR = 2
QUAD = 4
WIDE = QUAD * HEAD_DIM
FAR = 1e15
VMEM_BYTES = 61 * 1024 * 1024
SLOPES = [2.0 ** (-8.0 * (h + 1.0) / HEADS) for h in range(HEADS)]
SCALE = 1.0 / math.sqrt(HEAD_DIM)
F32 = jnp.float32
BF16 = jnp.bfloat16
SMALL_COST = pl.CostEstimate(flops=1, bytes_accessed=1, transcendentals=0)


def mm(left, right):
    return jnp.dot(left, right, preferred_element_type=F32)


def mm_t(left, right):
    return lax.dot_general(left, right, (((1,), (1,)), ((), ())), preferred_element_type=F32)


def t_mm(left, right):
    return lax.dot_general(left, right, (((0,), (0,)), ((), ())), preferred_element_type=F32)


def rows_of(ref):
    value = ref[...].astype(F32)
    return value.reshape(value.shape[0] * value.shape[1], value.shape[2])


def put_rows(ref, value):
    slots = ref.shape[1]
    for i in range(ref.shape[0]):
        ref[i] = value[i * slots : (i + 1) * slots].astype(ref.dtype)


def norm(values):
    centre = values - jnp.mean(values, axis=-1, keepdims=True)
    inverse = lax.rsqrt(jnp.mean(centre * centre, axis=-1, keepdims=True) + 1e-6)
    return centre * inverse, inverse


def norm_back(grad, scaled, inverse, gain):
    weighted = grad * gain
    return inverse * (
        weighted
        - jnp.mean(weighted, axis=-1, keepdims=True)
        - scaled * jnp.mean(weighted * scaled, axis=-1, keepdims=True)
    )


def column_sum(values):
    return jnp.sum(values, axis=0, keepdims=True)


def head_masks(dtype):
    lane = lax.broadcasted_iota(jnp.int32, (1, WIDE), 1) // HEAD_DIM
    return [(lane == h).astype(F32).astype(dtype) for h in range(QUAD)]


def as_column(row, slots):
    n = row.shape[1]
    same = lax.broadcasted_iota(jnp.int32, (slots, n), 0) == lax.broadcasted_iota(
        jnp.int32, (slots, n), 1
    )
    return jnp.sum(jnp.where(same, jnp.broadcast_to(row, (slots, n)), 0.0), axis=1, keepdims=True)


def distances(query_pos, key_pos, slots, keys):
    delta_row = as_column(query_pos[0:1], slots) - key_pos[0:1, :keys]
    delta_column = as_column(query_pos[1:2], slots) - key_pos[1:2, :keys]
    return jnp.sqrt(delta_row * delta_row + delta_column * delta_column)


def stacked(block, keys, masks):
    slots = block.shape[0]
    if keys <= slots:
        part = block[:keys]
    else:
        part = jnp.concatenate(
            (block.astype(F32), jnp.zeros((keys - slots, block.shape[1]), F32)), axis=0
        ).astype(BF16)
    return jnp.concatenate([part * m for m in masks], axis=0)


def attend(i, keys, q_of, k_of, v_of, query_pos, key_pos, p_ref, o_ref):
    slots = o_ref.shape[1]
    dist = distances(query_pos, key_pos, slots, keys)
    masks = head_masks(BF16)
    for g in range(HEADS // QUAD):
        q = q_of(g) * jnp.asarray(SCALE, BF16)
        scores = mm_t(q, stacked(k_of(g), keys, masks))
        parts = []
        for h in range(QUAD):
            s = scores[:, h * keys : (h + 1) * keys] - SLOPES[g * QUAD + h] * dist
            e = jnp.exp(s - jnp.max(s, axis=1, keepdims=True))
            parts.append((e * (1.0 / jnp.sum(e, axis=1, keepdims=True))).astype(BF16))
        p = jnp.concatenate(parts, axis=1)
        p_ref[i, :, g * QUAD * keys : (g + 1) * QUAD * keys] = p
        o_ref[i, :, g * WIDE : (g + 1) * WIDE] = mm(p, stacked(v_of(g), keys, masks)).astype(BF16)


def attend_back(i, keys, q_of, k_of, v_of, do_of, p_ref, put_dq, put_dk, put_dv, slots):
    masks = head_masks(BF16)
    wide_masks = head_masks(F32)

    def gathered(product):
        total = sum(product[h * keys : (h + 1) * keys] * wide_masks[h] for h in range(QUAD))
        if keys >= slots:
            return total[:slots]
        return jnp.concatenate((total, jnp.zeros((slots - keys, WIDE), F32)), axis=0)

    for g in range(HEADS // QUAD):
        q, do = q_of(g), do_of(g)
        keys_stack = stacked(k_of(g), keys, masks)
        dp = mm_t(do, stacked(v_of(g), keys, masks))
        p = p_ref[i, :, g * QUAD * keys : (g + 1) * QUAD * keys]
        parts = []
        for h in range(QUAD):
            ph = p[:, h * keys : (h + 1) * keys].astype(F32)
            t = ph * dp[:, h * keys : (h + 1) * keys]
            parts.append((t - ph * jnp.sum(t, axis=1, keepdims=True)).astype(BF16))
        ds = jnp.concatenate(parts, axis=1)
        put_dv(g, gathered(t_mm(p, do)).astype(BF16))
        put_dq(g, (mm(ds, keys_stack) * SCALE).astype(BF16))
        put_dk(g, (gathered(t_mm(ds, q)) * SCALE).astype(BF16))


def by_count(count, slots, work):
    small = min(slots, 128)
    pl.when(count <= small)(lambda: work(small))
    if slots > small:
        pl.when(count > small)(lambda: work(256))


def gelu_parts(u):
    size = jnp.abs(u)
    t = 1.0 / (1.0 + (0.3275911 / math.sqrt(2.0)) * size)
    poly = 0.5 * 1.061405429
    for c in (-1.453152027, 1.421413741, -0.284496736, 0.254829592):
        poly = poly * t + 0.5 * c
    bell = jnp.exp(-0.5 * (u * u))
    tail = poly * t * bell
    phi_cap = jnp.where(u >= 0.0, 1.0 - tail, tail)
    return u * phi_cap, phi_cap + u * (bell * (1.0 / math.sqrt(2.0 * math.pi)))


def live_rows(counts, slots):
    slot = lax.broadcasted_iota(jnp.int32, (slots, 1), 0)
    return jnp.concatenate([(slot < c).astype(F32) for c in counts], axis=0)


def self_forward(
    base, ready, count, x_ref, pos_ref, gain_ref, shift_ref, qkv_w, out_w, q_w,
    h1_ref, qkv_ref, p_ref, o_ref, x1_ref, h2_ref, q2_ref,
):
    step = pl.program_id(0)
    pair, slots, width = x_ref.shape
    x = rows_of(x_ref)
    scaled, _ = norm(x)
    h1 = (scaled * gain_ref[...].astype(F32)[0:1] + shift_ref[...].astype(F32)[0:1]).astype(BF16)
    put_rows(h1_ref, h1.astype(F32))
    put_rows(qkv_ref, mm(h1, qkv_w[...]))
    for i in range(pair):

        def block(kind, i=i):
            return lambda g: qkv_ref[i, :, kind * width + g * WIDE : kind * width + (g + 1) * WIDE]

        by_count(
            count[base + step * pair + i],
            slots,
            lambda keys, i=i, block=block: attend(
                i, keys, block(0), block(1), block(2), pos_ref[i], pos_ref[i], p_ref, o_ref
            ),
        )
    ready()
    x1 = x + mm(rows_of(o_ref).astype(BF16), out_w[...])
    put_rows(x1_ref, x1)
    scaled, _ = norm(x1)
    h2 = (scaled * gain_ref[...].astype(F32)[1:2] + shift_ref[...].astype(F32)[1:2]).astype(BF16)
    put_rows(h2_ref, h2.astype(F32))
    put_rows(q2_ref, mm(h2, q_w[...]))


def cross_and_mlp(
    base, ready, count, other_count, x1_ref, q2_ref, opt_ref, dy_ref, pos_ref, other_pos_ref, gain_ref, shift_ref,
    kv_w, out_w, in_w, in_b, mo_w, mo_b,
    mixed_ref, kv_ref, p_ref, o_ref, h3_ref, g_ref, du_ref, dm_ref, dx2_ref, sums_ref, in_sums_ref,
):
    step = pl.program_id(0)
    pair, slots, width = x1_ref.shape
    hidden = in_w.shape[1]
    put_rows(kv_ref, mm(rows_of(opt_ref).astype(BF16), kv_w[...]))
    for i in range(pair):

        def block(ref, kind, i=i):
            return lambda g: ref[i, :, kind * width + g * WIDE : kind * width + (g + 1) * WIDE]

        by_count(
            other_count[base + step * pair + i],
            slots,
            lambda keys, i=i, block=block: attend(
                i, keys, block(q2_ref, 0), block(kv_ref, 0), block(kv_ref, 1),
                pos_ref[i], other_pos_ref[i], p_ref, o_ref,
            ),
        )
    ready()
    x2 = rows_of(x1_ref) + mm(rows_of(o_ref).astype(BF16), out_w[...])
    scaled, inverse = norm(x2)
    gain = gain_ref[...].astype(F32)[2:3]
    h3 = (scaled * gain + shift_ref[...].astype(F32)[2:3]).astype(BF16)
    put_rows(h3_ref, h3.astype(F32))
    live = live_rows([count[base + step * pair + i] for i in range(pair)], slots)
    dy = rows_of(dy_ref) * live
    dm = dy.astype(BF16)
    put_rows(dm_ref, dy)
    chunk = 768
    g_parts, du_parts, in_sums = [], [], []
    for j in range(hidden // chunk):
        cols = slice(j * chunk, (j + 1) * chunk)
        u = mm(h3, in_w[:, cols]) + in_b[0:1, cols]
        dg = mm_t(dm, mo_w[cols, :]).astype(BF16).astype(F32)
        g, slope = gelu_parts(u)
        du = dg * slope
        for i in range(pair):
            rows = slice(i * slots, (i + 1) * slots)
            g_ref[i, :, cols] = g[rows].astype(BF16)
            du_ref[i, :, cols] = du[rows].astype(BF16)
        g_parts.append(g.astype(BF16))
        du_parts.append(du.astype(BF16))
        in_sums.append(column_sum(du.astype(BF16).astype(F32)))
    y = x2 + (mm(jnp.concatenate(g_parts, axis=1), mo_w[...]) + mo_b[0:1])
    put_rows(mixed_ref, y * live)
    dh3 = mm_t(jnp.concatenate(du_parts, axis=1), in_w[...])
    put_rows(dx2_ref, dy + norm_back(dh3, scaled, inverse, gain))
    sums = jnp.concatenate((column_sum(dh3 * scaled), column_sum(dh3), column_sum(dy)), axis=0)
    in_sums = jnp.concatenate(in_sums, axis=1)

    @pl.when(step == 0)
    def _():
        sums_ref[...] = sums
        in_sums_ref[...] = in_sums

    @pl.when(step > 0)
    def _():
        sums_ref[...] += sums
        in_sums_ref[...] += in_sums


def cross_back(
    base, ready, other_count, dx2_ref, x1_ref, q2_ref, kv_ref, p_ref, gain_ref, out_w, q_w, kv_w,
    da2_ref, dq2_ref, dkv_ref, og_ref, dx1_ref, sums_ref, do_ref,
):
    step = pl.program_id(0)
    pair, slots, width = x1_ref.shape
    dx2 = rows_of(dx2_ref)
    da2 = dx2.astype(BF16)
    put_rows(da2_ref, dx2)
    put_rows(do_ref, mm_t(da2, out_w[...]))
    for i in range(pair):

        def block(ref, kind, i=i):
            return lambda g: ref[i, :, kind * width + g * WIDE : kind * width + (g + 1) * WIDE]

        def put(ref, kind, i=i):
            def store(g, value):
                ref[i, :, kind * width + g * WIDE : kind * width + (g + 1) * WIDE] = value

            return store

        by_count(
            other_count[base + step * pair + i],
            slots,
            lambda keys, i=i, block=block, put=put: attend_back(
                i, keys, block(q2_ref, 0), block(kv_ref, 0), block(kv_ref, 1), block(do_ref, 0),
                p_ref, put(dq2_ref, 0), put(dkv_ref, 0), put(dkv_ref, 1), slots,
            ),
        )
    ready()
    put_rows(og_ref, mm_t(rows_of(dkv_ref).astype(BF16), kv_w[...]))
    dh2 = mm_t(rows_of(dq2_ref).astype(BF16), q_w[...])
    scaled, inverse = norm(rows_of(x1_ref))
    put_rows(dx1_ref, dx2 + norm_back(dh2, scaled, inverse, gain_ref[...].astype(F32)[1:2]))
    sums = jnp.concatenate((column_sum(dh2 * scaled), column_sum(dh2)), axis=0)

    @pl.when(step == 0)
    def _():
        sums_ref[...] = sums

    @pl.when(step > 0)
    def _():
        sums_ref[...] += sums


def self_back(
    base, ready, count, dx1_ref, x_ref, qkv_ref, p_ref, gain_ref, out_w, qkv_w,
    dqkv_ref, dx_ref, sums_ref, do_ref,
):
    step = pl.program_id(0)
    pair, slots, width = x_ref.shape
    dx1 = rows_of(dx1_ref)
    da1 = dx1.astype(BF16)
    put_rows(do_ref, mm_t(da1, out_w[...]))
    for i in range(pair):

        def block(ref, kind, i=i):
            return lambda g: ref[i, :, kind * width + g * WIDE : kind * width + (g + 1) * WIDE]

        def put(ref, kind, i=i):
            def store(g, value):
                ref[i, :, kind * width + g * WIDE : kind * width + (g + 1) * WIDE] = value

            return store

        by_count(
            count[base + step * pair + i],
            slots,
            lambda keys, i=i, block=block, put=put: attend_back(
                i, keys, block(qkv_ref, 0), block(qkv_ref, 1), block(qkv_ref, 2), block(do_ref, 0),
                p_ref, put(dqkv_ref, 0), put(dqkv_ref, 1), put(dqkv_ref, 2), slots,
            ),
        )
    ready()
    dh1 = mm_t(rows_of(dqkv_ref).astype(BF16), qkv_w[...])
    scaled, inverse = norm(rows_of(x_ref))
    put_rows(dx_ref, dx1 + norm_back(dh1, scaled, inverse, gain_ref[...].astype(F32)[0:1]))
    sums = jnp.concatenate((column_sum(dh1 * scaled), column_sum(dh1)), axis=0)

    @pl.when(step == 0)
    def _():
        sums_ref[...] = sums

    @pl.when(step > 0)
    def _():
        sums_ref[...] += sums


def take_images(source, place, *refs):
    out = refs[-1]
    together = out.shape[0]
    each = (len(refs) - 1) // together
    for k in range(together):
        chosen = source[pl.program_id(0) * together + k]
        for r in range(each):

            @pl.when(chosen == r)
            def _(ref=refs[k * each + r], k=k):
                out[k] = ref[0]


def split_first(core, bits, *refs):
    outs = refs[-2 * PARTS :]
    count = (len(refs) - 2 * PARTS) // (4 * PARTS)
    for place, out in enumerate(outs):
        column = 0
        for k in range(count):
            first = (place * count + k) * 2
            value = refs[first][...].astype(F32) + refs[first + 1][...].astype(F32)
            chunk, r, _ = out.shape
            for j in range(chunk):
                out[j, :, column : column + value.shape[1]] = value[j * r : (j + 1) * r].astype(out.dtype)
            column += value.shape[1]


def add_blocks(bits, *refs):
    third = len(refs) // 3
    for one, other, out in zip(refs[:third], refs[third : 2 * third], refs[2 * third :]):
        out[...] = (one[...].astype(F32) + other[...].astype(F32)).astype(out.dtype)


def unpack_blocks(core, bits, *refs):
    outs = refs[4 * PARTS :]
    here = pl.program_id(0) == core[0]

    for p in range(PARTS):
        own = pl.program_id(1) == bits[p]
        for where, first in ((here, 0), (jnp.logical_not(here), 2)):
            for whose, second in ((own, 0), (jnp.logical_not(own), 1)):

                @pl.when(jnp.logical_and(where, whose))
                def _(source=refs[(first + second) * PARTS + p], p=p):
                    column = 0
                    for out in outs:
                        out[0, p, 0] = source[:, :, column : column + out.shape[-1]]
                        column += out.shape[-1]


def merge_blocks(bits, *refs):
    third = len(refs) // 3
    half = pl.program_id(0)
    for p, (one, other, out) in enumerate(zip(refs[:third], refs[third : 2 * third], refs[2 * third :])):

        @pl.when(half == bits[p])
        def _(one=one, out=out):
            out[...] = one[...].reshape(out.shape)

        @pl.when(half != bits[p])
        def _(other=other, out=out):
            out[...] = other[...].reshape(out.shape)


class Thread:
    def __init__(self, arrays):
        self.arrays = tuple(arrays)


def passing(after):
    threads = [x for x in after if isinstance(x, Thread)]
    waits = [x for x in after if not isinstance(x, Thread)]
    through = [x for t in threads for x in t.arrays]

    def hand_back(results):
        results = list(results)
        for t in threads:
            t.arrays, results = tuple(results[: len(t.arrays)]), results[len(t.arrays) :]

    return waits, through, hand_back


def images_call(kernel, scalars, arrays, whole, outs, sums, scratch, flops, name, part=(0, 1), into=None, after=(), late=()):
    images = arrays[0].shape[0]
    pair = PAIR if images % PAIR == 0 else 1
    steps = images // pair // part[1]
    first = part[0] * steps
    into = into or ()

    def split_spec(shape):
        rank = len(shape)
        return pl.BlockSpec((pair,) + tuple(shape[1:]), lambda i, *s: (i + first,) + (0,) * (rank - 1))

    def whole_spec(shape):
        rank = len(shape)
        return pl.BlockSpec(tuple(shape), lambda i, *s: (0,) * rank, pipeline_mode=pl.Buffered(1))

    out_shapes = [jax.ShapeDtypeStruct((images,) + tail, dtype) for tail, dtype in outs]
    sum_shapes = [jax.ShapeDtypeStruct(shape, F32) for shape in sums]
    waits, through, hand_back = passing(after)
    free = [*waits, *into, *through]
    n_used = len(scalars) + len(arrays) + len(whole)
    n_outs = len(out_shapes) + len(sum_shapes)
    shapes = out_shapes + sum_shapes + [jax.ShapeDtypeStruct(x.shape, x.dtype) for x in through]

    scratch_shapes = [pltpu.VMEM((pair,) + tail, dtype) for tail, dtype in scratch]
    scratch_shapes += [pltpu.VMEM(whole[k].shape, whole[k].dtype) for k in late]
    scratch_shapes += [pltpu.SemaphoreType.DMA((max(1, len(late)),))]

    def run(*refs):
        refs, rest = list(refs[:n_used]), refs[n_used + len(free) :]
        outs_, scratch_ = rest[:n_outs], rest[n_outs + len(through) :]
        sem, held = scratch_[-1], scratch_[len(scratch) : -1]
        begin = pl.program_id(0) == 0
        copies = []
        for k, (w, inside) in enumerate(zip(late, held)):
            place = len(scalars) + len(arrays) + w
            copies.append(pltpu.make_async_copy(refs[place], inside, sem.at[k]))
            refs[place] = inside

        @pl.when(begin)
        def _():
            for copy in copies:
                copy.start()

        def ready():
            @pl.when(begin)
            def _():
                for copy in copies:
                    copy.wait()

        kernel(first * pair, ready, *refs, *outs_, *scratch_[: len(scratch)])

    aliases = {n_used + len(waits) + k: k for k in range(len(into))}
    aliases |= {n_used + len(waits) + len(into) + k: n_outs + k for k in range(len(through))}
    results = pl.pallas_call(
        run,
        grid_spec=pltpu.PrefetchScalarGridSpec(
            num_scalar_prefetch=len(scalars),
            grid=(steps,),
            in_specs=[split_spec(a.shape) for a in arrays]
            + [
                pl.BlockSpec(memory_space=pl.ANY) if k in late else whole_spec(a.shape) for k, a in enumerate(whole)
            ]
            + [pl.BlockSpec(memory_space=pl.ANY)] * len(free),
            out_specs=[split_spec(o.shape) for o in out_shapes]
            + [pl.BlockSpec(s.shape, lambda i, *_: (0, 0)) for s in sum_shapes]
            + [pl.BlockSpec(memory_space=pl.ANY)] * len(through),
            scratch_shapes=scratch_shapes,
        ),
        out_shape=shapes,
        input_output_aliases=aliases,
        compiler_params=pltpu.CompilerParams(vmem_limit_bytes=VMEM_BYTES),
        cost_estimate=SMALL_COST,
        name=name,
    )(*scalars, *arrays, *whole, *free)
    hand_back(results[n_outs:])
    return results[:n_outs]


def take_call(source, place, sources):
    shape = sources[0].shape
    together = TOGETHER if shape[0] % TOGETHER == 0 else 1

    def spec(k, r):
        def index(j, source, place):
            image = j * together + k
            return (jnp.where(source[image] == r, place[image], 0), 0, 0)

        return pl.BlockSpec((1,) + shape[1:], index)

    return pl.pallas_call(
        take_images,
        grid_spec=pltpu.PrefetchScalarGridSpec(
            num_scalar_prefetch=2,
            grid=(shape[0] // together,),
            in_specs=[spec(k, r) for k in range(together) for r in range(len(sources))],
            out_specs=pl.BlockSpec((together,) + shape[1:], lambda j, source, place: (j, 0, 0)),
        ),
        compiler_params=pltpu.CompilerParams(vmem_limit_bytes=VMEM_BYTES),
        out_shape=jax.ShapeDtypeStruct(shape, sources[0].dtype),
        cost_estimate=SMALL_COST,
        name="take_images",
    )(source, place, *(sources * together))


def plain_call(kernel, scalars, grid, ins, outs, name, after=()):
    waits, through, hand_back = passing(after)
    free = [*waits, *through]
    n_used, n_outs = len(scalars) + len(ins), len(outs)

    def run(*refs):
        refs, rest = refs[:n_used], refs[n_used + len(free) :]
        kernel(*refs, *rest[:n_outs])

    results = pl.pallas_call(
        run,
        grid_spec=pltpu.PrefetchScalarGridSpec(
            num_scalar_prefetch=len(scalars),
            grid=grid,
            in_specs=[pl.BlockSpec(block, index) for _, block, index in ins]
            + [pl.BlockSpec(memory_space=pl.ANY)] * len(free),
            out_specs=[pl.BlockSpec(block, index) for _, block, index in outs]
            + [pl.BlockSpec(memory_space=pl.ANY)] * len(through),
        ),
        out_shape=[jax.ShapeDtypeStruct(shape, BF16) for shape, _, _ in outs]
        + [jax.ShapeDtypeStruct(x.shape, x.dtype) for x in through],
        input_output_aliases={n_used + len(waits) + k: n_outs + k for k in range(len(through))},
        compiler_params=pltpu.CompilerParams(vmem_limit_bytes=VMEM_BYTES),
        cost_estimate=SMALL_COST,
        name=name,
    )(*scalars, *[a for a, _, _ in ins], *free)
    hand_back(results[n_outs:])
    return results[:n_outs]


def bit_of(axis_name, bit):
    return (lax.axis_index(axis_name) // bit) % 2


def own_place():
    return lax.axis_index("chip") * 2 + lax.axis_index("core")


PARTS = 3
TOGETHER = 4


def sum_links(turn):
    chip, dp = lax.axis_size("chip"), lax.axis_size("dp")
    links = [("chip", 2**i) for i in reversed(range(chip.bit_length() - 1))]
    links += [("dp", 2**i) for i in range(dp.bit_length() - 1)]
    return links[turn:PARTS] + links[:turn] + links[PARTS:]


def sum_levels():
    orders = [sum_links(p) for p in range(PARTS)]
    return [list(level) for level in zip(*orders)]


def take_own(refs_every, *outs):
    one, two = outs
    for j in range(refs_every.shape[0]):
        r = refs_every.shape[2]
        one[j] = refs_every[j, 0]
        wide = two.shape[3]
        for k in range(two.shape[1]):
            two[j, k] = refs_every[j, 1, :, k * wide : (k + 1) * wide]


def total_of_pieces(products):
    core = bit_of("core", 1)
    orders = [sum_links(0)[k:] + sum_links(0)[:k] for k in range(len(products))]
    chip, dp = lax.axis_size("chip").bit_length() - 1, lax.axis_size("dp").bit_length() - 1
    links = [("dp", 2**i) for i in reversed(range(dp))] + [("chip", 2**i) for i in reversed(range(chip))]
    got = [flip(product(1 - core).astype(BF16), "core", 1) for product in products]
    keep, shapes = [], []
    for product, more in zip(products, got):
        kept = (product(core) + more.astype(F32)).astype(BF16)
        shapes.append((2 * kept.shape[0], kept.shape[1]))
        keep.append(kept.reshape((2,) * len(links) + (kept.shape[0] // 2 ** len(links), kept.shape[1])))
    for k in range(len(links)):
        send = []
        for m, order in enumerate(orders):
            b, axis = bit_of(*order[k]), links.index(order[k])
            send.append(lax.dynamic_slice_in_dim(keep[m], 1 - b, 1, axis))
            keep[m] = lax.dynamic_slice_in_dim(keep[m], b, 1, axis)
        got = [flip(x, *order[k]) for x, order in zip(send, orders)]
        keep = yield tuple(send) + (Thread(keep),)
        keep = [(one.astype(F32) + more.astype(F32)).astype(BF16) for one, more in zip(keep, got)]
    (r, wide), (rows, columns) = sorted(x.shape[-2:] for x in keep)
    parts = rows // r
    pieces = []
    for x in keep:
        x = x.reshape(-1, r, x.shape[-1])
        pieces.append(x.swapaxes(0, 1).reshape(1, r, wide))
    pieces = jnp.stack(pieces, axis=1)
    every = lax.all_gather(pieces, ("core", "dp", "chip"), axis=0, tiled=True)
    yield (pieces,)
    count = every.shape[0]
    chunk = 4
    tall = [m for m, x in enumerate(keep) if x.shape[-2] != r]
    tall = tall[0] if tall else 1
    one, two = pl.pallas_call(
        take_own,
        grid=(count // chunk,),
        in_specs=[pl.BlockSpec((chunk, 2, r, wide), lambda i: (i, 0, 0, 0))],
        out_specs=[
            pl.BlockSpec((chunk, r, wide), lambda i: (i, 0, 0)),
            pl.BlockSpec((chunk, parts, r, columns), lambda i: (i, 0, 0, 0)),
        ],
        out_shape=[
            jax.ShapeDtypeStruct((count, r, wide), BF16),
            jax.ShapeDtypeStruct((count, parts, r, columns), BF16),
        ],
        compiler_params=pltpu.CompilerParams(vmem_limit_bytes=VMEM_BYTES),
        cost_estimate=SMALL_COST,
        name="take_own",
    )(every)
    yield [one.reshape(shapes[0]), two.reshape(shapes[1])]


def exchange(arrays, level):
    if len(set(level)) == 1:
        got = flip(jnp.concatenate(arrays, axis=0), *level[0])
        return [(got, p * arrays[0].shape[0]) for p in range(len(arrays))]
    return [(flip(x, *link), 0) for x, link in zip(arrays, level)]


def total_by_halves(products):
    levels = sum_levels()
    core = bit_of("core", 1)

    def scalars(level):
        return jnp.stack([bit_of(*link) for link in level]).astype(jnp.int32)

    got = [flip(product(1 - core).astype(BF16), "core", 1) for product in products]
    keep = [product(core).astype(BF16) for product in products]
    after = yield (keep[0],)
    rows = 2 * keep[0].shape[0]
    widths = [m.shape[1] for m in keep]
    wide = sum(widths)
    n = 2 ** len(levels)
    r = rows // (2 * PARTS * n)
    half = n // 2
    chunk = min(half, max(1, 16 // r))
    core = core[None].astype(jnp.int32)
    ins = []
    for other in (True, False):
        for p in range(PARTS):
            for one, more in zip(keep, got):

                def index(i, core, bits, p=p, other=other):
                    b = 1 - bits[p] if other else bits[p]
                    return ((p * n + b * half) // chunk + i, 0)

                ins += [(x, (chunk * r, x.shape[1]), index) for x in (one, more)]
    outs = [((half, r, wide), (chunk, r, wide), lambda i, core, bits: (i, 0, 0))] * (2 * PARTS)
    done = plain_call(split_first, (core, scalars(levels[0])), (half // chunk,), ins, outs, "split_first", after)
    for k, level in enumerate(levels):
        send, keep = done[:PARTS], done[PARTS:]
        got = exchange(send, level)
        after = yield (keep[0],)
        n //= 2
        if k + 1 == len(levels):
            break
        half = n // 2
        chunk = min(half, max(1, 16 // r))
        ones, others = [], []
        for other in (True, False):
            for p in range(PARTS):

                def index(i, bits, p=p, other=other, first=0):
                    b = 1 - bits[p] if other else bits[p]
                    return ((first + b * half) // chunk + i, 0, 0)

                ones.append((keep[p], (chunk, r, wide), index))
                others.append((got[p][0], (chunk, r, wide), partial(index, first=got[p][1])))
        outs = [((half, r, wide), (chunk, r, wide), lambda i, bits: (i, 0, 0))] * (2 * PARTS)
        done = plain_call(add_blocks, (scalars(levels[k + 1]),), (half // chunk,), ones + others, outs, "add_blocks", after)
    ins = [(x, (1, r, wide), lambda i, bits, f=f: (f, 0, 0)) for x, f in [(x, 0) for x in keep] + got]
    have = plain_call(
        add_blocks, (core,), (1,), ins, [((1, r, wide), (1, r, wide), lambda i, bits: (0, 0, 0))] * PARTS, "add_blocks", after
    )
    for level in reversed(levels):
        got = exchange(have, level)
        if level is levels[0]:
            got = [x for x, _ in got]
            break
        after = yield (have[0],)
        ins = [(x, (n, r, wide), lambda i, bits, f=f // n: (f, 0, 0)) for x, f in [(x, 0) for x in have] + got]
        outs = [((2 * n, r, wide), (n, r, wide), lambda i, bits: (i, 0, 0))] * PARTS
        have = plain_call(merge_blocks, (scalars(level),), (2,), ins, outs, "merge_blocks", after)
        n *= 2
    other_have = [flip(x, "core", 1) for x in have]
    other_got = [flip(x, "core", 1) for x in got]
    after = yield (have[0],)
    sums = plain_call(
        unpack_blocks,
        (core, scalars(levels[0])),
        (2, 2),
        [(x, (n, r, wide), lambda h, b, core, bits: (0, 0, 0)) for x in (*have, *got, *other_have, *other_got)],
        [((2, PARTS, 2, n, r, w), (1, PARTS, 1, n, r, w), lambda h, b, core, bits: (h, 0, b, 0, 0, 0)) for w in widths],
        "unpack_blocks",
        after,
    )
    yield [x.reshape(rows, w) for x, w in zip(sums, widths)]


def half_of_rows(left, right):
    def product(half):
        flat = left.reshape(-1, left.shape[-1])
        wide = flat.shape[1] // 2
        return row_product(lax.dynamic_slice_in_dim(flat, half * wide, wide, 1), right)

    return product


def half_of(values):
    rows = values.shape[0] // 2
    return lambda half: lax.dynamic_slice_in_dim(values, half * rows, rows, 0)


def positions(patches, count):
    slots = patches.shape[1]
    live = jnp.arange(slots, dtype=jnp.int32)[None, :] < count[:, None]
    row = jnp.where(live, (patches // GRID).astype(F32), FAR)
    column = (patches % GRID).astype(F32)
    pos = jnp.stack((row, column), axis=1)
    return jnp.pad(pos, ((0, 0), (0, 0), (0, 256 - slots)), constant_values=FAR)


def flip(values, axis_name, bit):
    size = lax.axis_size(axis_name)
    return lax.ppermute(values, axis_name, [(i, i ^ bit) for i in range(size)])


def gather_far(values):
    reach = {0: values}
    bit = lax.axis_size("chip") // 2
    while bit:
        for r in list(reach):
            reach[r ^ (2 * bit)] = flip(reach[r], "chip", bit)
        bit //= 2
    return reach


def gather_near(reach):
    both = {r: x for r, x in reach.items()}
    for r, x in reach.items():
        both[r ^ 1] = flip(x, "core", 1)
    return [both[r] for r in range(len(both))]


def row_product(left, right):
    return lax.dot_general(
        left.reshape(-1, left.shape[-1]),
        right.reshape(-1, right.shape[-1]),
        (((0,), (0,)), ((), ())),
        preferred_element_type=F32,
    )


def total(values):
    return lax.psum(values, ("dp", "chip", "core"))


def body(
    radar, optical, cotangent, radar_ratio, optical_ratio, radar_patches, optical_patches, pairing,
    norm_gain, norm_bias, self_qkv, self_out, cross_q, cross_kv, cross_out,
    mlp_in, mlp_in_bias, mlp_out, mlp_out_bias,
):
    images, slots, width = radar.shape
    hidden = mlp_in.shape[1]
    me = own_place()
    start = me * images
    gains, shifts = norm_gain, norm_bias

    def own(values):
        return lax.dynamic_slice_in_dim(values, start, images, 0)


    radar_count = GRID * GRID * (100 - own(radar_ratio)) // 100
    partner = own(pairing)
    other_count = (GRID * GRID * (100 - optical_ratio) // 100)[partner]
    pos = positions(own(radar_patches), radar_count)
    other_pos = positions(optical_patches[partner], other_count)

    rows = images * slots
    wide_p = HEADS * 256 if slots > 128 else HEADS * slots
    attention = 2 * images * HEADS * slots * 256 * HEAD_DIM
    h1, qkv, p1, o1, x1, h2, q2 = images_call(
        self_forward,
        (radar_count,),
        (radar, pos),
        (gains, shifts, self_qkv, self_out, cross_q),
        [
            ((slots, width), BF16),
            ((slots, 3 * width), BF16),
            ((slots, wide_p), BF16),
            ((slots, width), BF16),
            ((slots, width), F32),
            ((slots, width), BF16),
            ((slots, width), BF16),
        ],
        [],
        [],
        2 * rows * width * width * 5 + 2 * attention,
        "self_forward",
        late=(3, 4),
    )
    far, x1 = lax.optimization_barrier((gather_far(optical), x1))
    optical_blocks = gather_near(far)
    paired = take_call(partner // images ^ me, partner % images, optical_blocks)
    mixed, kv, p2, o2, h3, g, du, dm, dx2, sums3, in_sums = images_call(
        cross_and_mlp,
        (radar_count, other_count),
        (x1, q2, paired, cotangent, pos, other_pos),
        (
            gains, shifts, cross_kv, cross_out, mlp_in, mlp_in_bias.astype(F32)[None],
            mlp_out, mlp_out_bias.astype(F32)[None],
        ),
        [
            ((slots, width), BF16),
            ((slots, 2 * width), BF16),
            ((slots, wide_p), BF16),
            ((slots, width), BF16),
            ((slots, width), BF16),
            ((slots, hidden), BF16),
            ((slots, hidden), BF16),
            ((slots, width), BF16),
            ((slots, width), F32),
        ],
        [(3, width), (1, hidden)],
        [],
        2 * rows * width * (3 * width + 4 * hidden) + 2 * attention,
        "cross_and_mlp",
        late=(3, 4, 6),
    )
    first = total_of_pieces((half_of_rows(h3, du), half_of_rows(g, dm)))
    before_cross = next(first)
    da2, dq2, dkv, og, dx1, sums2 = images_call(
        cross_back,
        (other_count,),
        (dx2, x1, q2, kv, p2),
        (gains, cross_out, cross_q, cross_kv),
        [
            ((slots, width), BF16),
            ((slots, width), BF16),
            ((slots, 2 * width), BF16),
            ((slots, width), BF16),
            ((slots, width), F32),
        ],
        [(2, width)],
        [((slots, width), BF16)],
        2 * rows * width * width * 4 + 4 * attention,
        "cross_back",
        late=(2, 3),
        after=before_cross,
    )
    second = [
        half_of_rows(o2, da2), half_of_rows(h2, dq2), half_of_rows(paired, dkv), half_of_rows(o1, dx1.astype(BF16))
    ]
    core = lax.axis_index("core")
    halves = [tuple(product(half).astype(BF16) for half in (1 - core, core)) for product in second]
    og_far = gather_far(og)

    def step_first(begun):
        return first.send(begun[-1].arrays) if isinstance(begun[-1], Thread) else next(first)

    begun = step_first(before_cross)
    scalars, arrays, whole = (radar_count,), (dx1, radar, qkv, p1), (gains, self_out, self_qkv)
    outs = [((slots, 3 * width), BF16), ((slots, width), BF16)]
    made = None
    for part in range(2):
        *made, sums = images_call(
            self_back, scalars, arrays, whole, outs, [(2, width)], [((slots, width), BF16)], 0, "self_back", late=(2,),
            part=(part, 2), into=made, after=begun + (sum(halves, ()) if part == 0 else ()) + (tuple(og_far[r] for r in og_far if r) if part == 1 else ()),
        )
        sums1 = sums if part == 0 else sums1 + sums
        begun = step_first(begun)
    after = tuple(x for x in begun if not isinstance(x, Thread))
    dqkv, radar_grad = made
    og_blocks = gather_near(og_far)
    inverse_pairing = own(jnp.argsort(pairing))
    optical_grad = take_call(inverse_pairing // images ^ me, inverse_pairing % images, og_blocks)
    small = jnp.concatenate((sums1, sums2, sums3, in_sums.reshape(-1, width)), axis=0)
    count = small.shape[0]
    small = jnp.pad(small.astype(BF16).T, ((0, 0), (0, 128 - count)))
    ready = [iter(pair) for pair in halves]
    second = [lambda half, pair=pair: next(pair) for pair in ready]
    while not isinstance(begun, list):
        begun = step_first(begun)
    grad_mlp_in, grad_mlp_out = begun
    last_round = 2 * len(sum_levels())
    rest = total_by_halves((*second, half_of_rows(h1, dqkv), half_of(small)))
    next(rest)
    rounds = 0
    while not isinstance(after, list):
        rounds += 1
        if rounds == 2:
            after = after + (optical_grad,)
        if rounds == last_round:
            after = after + (grad_mlp_in,)
        after = rest.send(after)
    grad_cross_out, grad_cross_q, grad_cross_kv, grad_self_out, grad_self_qkv, small = after
    small = small[:, :count].T
    gain_grads = jnp.stack((small[0], small[2], small[4]))
    shift_grads = jnp.stack((small[1], small[3], small[5]))
    grad_mlp_in_bias, grad_mlp_out_bias = small[7:].reshape(hidden), small[6]
    return (
        mixed, radar_grad, optical_grad, gain_grads.astype(BF16), shift_grads.astype(BF16),
        grad_self_qkv, grad_self_out, grad_cross_q, grad_cross_kv, grad_cross_out,
        grad_mlp_in, grad_mlp_in_bias.astype(BF16), grad_mlp_out, grad_mlp_out_bias.astype(BF16),
    )


def solution(mesh):
    dp, head = mesh.shape["dp"], mesh.shape["head"]
    mesh = jax.sharding.Mesh(mesh.devices.reshape(dp, head // 2, 2), ("dp", "chip", "core"))
    split, group, copied = P(("dp", "chip", "core"), None, None), P("dp"), P()
    return jax.shard_map(
        body,
        mesh=mesh,
        in_specs=(split,) * 3 + (group,) * 5 + (copied,) * 11,
        out_specs=(split,) * 3 + (copied,) * 11,
        check_vma=False,
    )
```
